512 devices in a mesh: dp: 16 (over x, y_hi, core), own: 32 (over z, y_lo).
Axes of the slice: x: 4, y: 8 (y_hi: 2, y_lo: 4; y = y_hi * 4 + y_lo), z: 8, core: 2. Of those that a mesh axis runs over, the one named last changes fastest.
Arguments:
- hidden_act: bfloat16 [65536, 12288], P(('dp', 'own')), may hold values from -1000 to 1000
- out_grad: bfloat16 [65536, 4096], P(('dp', 'own')), may hold values from -1000 to 1000
- weight_grad: bfloat16 [12288, 4096], P('own', 'dp'), may hold values from -6 to 6
- owner_a: int32 [96], replicated, may hold values from 0 to 95, each once
- owner_g: int32 [32], replicated, may hold values from 0 to 31, each once
Outputs:
- a_inverse: bfloat16 [96, 128, 128], P('own')
- g_inverse: bfloat16 [32, 128, 128], P('own')
- precond: float32 [12288, 4096], P('own', 'dp')
The draws below stay inside these ranges and needn't reach their ends.
Inputs may be any that keep to these rules, and one draw needn't show every extreme that they name: `owner_a`: slots s * 3 to s * 3 + 2 belong to index s of own; every slot holds exactly one block. `owner_g`: slots s * 1 to s + 1 - 1 belong to index s of own; every slot holds exactly one block.
All inputs are finite; a program needn't handle non-finite values. Where the reference program divides by a largest or mean magnitude, that divisor is 1e-20 or more.
Results may differ from the reference program's by a relative error of at most 0.0058.
Values may be sent and summed in bfloat16 or wider, within the bound.
A program may use at most 64 MiB of HBM per device.

```python
import math
import jax
import jax.numpy as jnp
from jax import lax

FFW = 12288
DW = 4096
BLK = 128
ITERS = 14
TOKENS = 65536
HA = 96
HG = 32


def shape_columns(key, noise_part, low_end, high_end):
    row_count, col_count = noise_part.shape
    subkeys = jax.random.split(key, 5)
    first_shared = jnp.repeat(jax.random.normal(subkeys[0], (row_count, col_count // BLK), jnp.float32), BLK, axis=1)
    second_shared = jnp.repeat(jax.random.normal(subkeys[1], (row_count, col_count // BLK), jnp.float32), BLK, axis=1)
    load_one = jax.random.normal(subkeys[2], (col_count,), jnp.float32)
    load_two = jax.random.normal(subkeys[3], (col_count,), jnp.float32)
    spread = jnp.exp(jax.random.uniform(subkeys[4], (col_count,), jnp.float32, math.log(low_end), math.log(high_end)))
    rising = jnp.sqrt(1.0 + 2.0 * jnp.arange(row_count, dtype=jnp.float32) / (row_count - 1))[:, None]
    mixed = rising * spread * (noise_part + load_one * first_shared + load_two * second_shared)
    return mixed.astype(jnp.bfloat16)


def draw_hidden_act(key, part):
    key = jax.random.fold_in(key, 11)
    noise_key, shape_key = jax.random.split(key)
    noise_part = jax.random.normal(noise_key, (TOKENS, FFW), jnp.float32)
    return shape_columns(shape_key, noise_part, 0.3, 3.0)


def draw_out_grad(key, part):
    key = jax.random.fold_in(key, 23)
    noise_key, shape_key = jax.random.split(key)
    noise_part = jax.random.normal(noise_key, (TOKENS, DW), jnp.float32)
    return shape_columns(shape_key, noise_part, 0.3, 3.0)


def steps_of(key, dims, cuts, smallest, largest):
    gain = 1.0
    for dim, shards_of in cuts:
        steps = jax.random.uniform(jax.random.fold_in(jax.random.fold_in(key, 6), dim), (shards_of,), jnp.float32, smallest / len(cuts), largest / len(cuts))
        gain = gain * jnp.repeat(jnp.exp(steps), dims[dim] // shards_of).reshape((-1,) + (1,) * (len(dims) - 1 - dim))
    return gain


def noise(own_key, shape, width, most, shards=(), held_as=jnp.bfloat16):
    factor_of = steps_of(own_key, shape, shards, -0.22, 0.18) if shards else 1.0
    array = jax.random.normal(own_key, shape, jnp.float32) * width * factor_of
    return jnp.minimum(jnp.maximum(array, -most), most).astype(held_as)


def setup_inputs(seed: int = 0) -> dict:
    streams_of = jax.random.split(jax.random.key(seed), 6)
    hidden_act = draw_hidden_act(jax.random.fold_in(streams_of[5], 71), 0)
    out_grad = draw_out_grad(jax.random.fold_in(streams_of[5], 71), 0)
    weight_grad = noise(streams_of[2], (FFW, DW), 1.0, 6.0, ((0, 32), (1, 16)))
    owner_a = jax.random.permutation(streams_of[3], HA).astype(jnp.int32)
    owner_g = jax.random.permutation(streams_of[4], HG).astype(jnp.int32)
    return {"hidden_act": hidden_act, "out_grad": out_grad, "weight_grad": weight_grad, "owner_a": owner_a, "owner_g": owner_g}


DAMPING = 0.05


def covariances(columns_all, count):
    def single(block_index):
        columns = lax.dynamic_slice_in_dim(columns_all, block_index * BLK, BLK, 1)
        return jnp.dot(columns.T, columns, preferred_element_type=jnp.float32)
    return lax.map(single, jnp.arange(count, dtype=jnp.int32))


def newton(factors):
    identity = jnp.eye(factors.shape[-1], dtype=jnp.float32)
    bound_row = jnp.max(jnp.sum(jnp.abs(factors), axis=2), axis=1)
    start = identity[None, :, :] / bound_row[:, None, None]

    def refine(step_index, current):
        product = jnp.einsum("sij,sjk->sik", factors, current, precision=lax.Precision.HIGHEST)
        return jnp.einsum("sij,sjk->sik", current, 2.0 * identity - product, precision=lax.Precision.HIGHEST)
    return lax.fori_loop(0, ITERS, refine, start)


def reference(hidden_act, out_grad, weight_grad, owner_a, owner_g):
    identity = jnp.eye(BLK, dtype=jnp.float32)
    factor_a = covariances(hidden_act, HA) / TOKENS + DAMPING * identity
    factor_g = covariances(out_grad, HG) / TOKENS + DAMPING * identity
    inv_a = newton(factor_a).astype(jnp.bfloat16)
    inv_g = newton(factor_g).astype(jnp.bfloat16)
    a_inverse = jnp.zeros_like(inv_a).at[owner_a].set(inv_a)
    g_inverse = jnp.zeros_like(inv_g).at[owner_g].set(inv_g)
    grad_rows = weight_grad.reshape(HA, BLK, DW).astype(jnp.float32)
    left_side = jnp.einsum("bij,bjc->bic", inv_a.astype(jnp.float32), grad_rows).astype(jnp.bfloat16)
    left_side = left_side.reshape(FFW, HG, BLK).astype(jnp.float32)
    precond = jnp.einsum("rcj,cjk->rck", left_side, inv_g.astype(jnp.float32)).reshape(FFW, DW)
    return a_inverse, g_inverse, precond
```

```python
import jax
import jax.numpy as jnp
from jax import lax
from jax.experimental import pallas as pl
from jax.experimental.pallas import tpu as pltpu
from jax.sharding import PartitionSpec as P

BLK = 128
ITERS = 14
DAMPING = 0.05
NX, NY, NZ, NYL = 4, 8, 8, 4
MESH = pl.DeviceIdType.MESH
F32 = jnp.float32
BF16 = jnp.bfloat16


def place():
    dp = lax.axis_index("dp")
    own = lax.axis_index("own")
    return dp // 4, ((dp // 2) % 2) * NYL + own % NYL, own // NYL, dp % 2


def device(x, y, z, c):
    return (x * 4 + (y // NYL) * 2 + c, z * NYL + y % NYL)


def send(src, dst, send_sem, recv_sem, to):
    copy = pltpu.make_async_remote_copy(
        src_ref=src, dst_ref=dst, send_sem=send_sem, recv_sem=recv_sem,
        device_id=to, device_id_type=MESH,
    )
    copy.start()


def arrived(ref, sem):
    pltpu.make_async_copy(ref, ref, sem).wait()


def gram_kernel(hid, grd, m_out, d_out,
                raw, ta, tb, tg, ra, rb, rg, a2, b2, g2, ra2, rb2, rg2, a3, x3, ra3, rx3, fin,
                s_loc, s_raw_s, s_raw_r, s_a, r_a, s_b, r_b, s_g, r_g,
                s_a2, r_a2, s_b2, r_b2, s_g2, r_g2, s_a3, r_a3, s_x3, r_x3, s_f, r_f):
    x, y, z, c = place()
    sib = device(x, y, z, 1 - c)

    barrier = pltpu.get_barrier_semaphore()
    pl.semaphore_signal(barrier, inc=1, device_id=sib, device_id_type=MESH)
    for j in range(1, NX):
        pl.semaphore_signal(barrier, inc=1, device_id=device((x + j) % NX, y, z, c), device_id_type=MESH)
    for j in range(1, NY):
        pl.semaphore_signal(barrier, inc=1, device_id=device(x, (y + j) % NY, z, c), device_id_type=MESH)
    for j in range(1, NZ):
        pl.semaphore_signal(barrier, inc=1, device_id=device(x, y, (z + j) % NZ, c), device_id_type=MESH)

    def local_parts(zz, core, rows):
        return (
            (hid.at[:, pl.ds(pl.multiple_of(6144 * core + 768 * zz, 128), 768)],
             raw.at[rows, pl.ds(pl.multiple_of(1024 * zz, 128), 768)]),
            (grd.at[:, pl.ds(pl.multiple_of(2048 * core + 256 * zz, 128), 256)],
             raw.at[rows, pl.ds(pl.multiple_of(1024 * zz + 768, 128), 256)]),
        )

    low, high = pl.ds(0, 128), pl.ds(128, 128)

    @pl.loop(0, NZ)
    def _(i):
        zz = (z + 1 + i) % NZ
        for k, (src, dst) in enumerate(local_parts(zz, c, low)):
            pltpu.make_async_copy(src, dst, s_loc.at[i, k]).start()

    pl.semaphore_wait(barrier, 1 + (NX - 1) + (NY - 1) + (NZ - 1))

    @pl.loop(0, NZ)
    def _(i):
        zz = (z + 1 + i) % NZ
        for k, (src, dst) in enumerate(local_parts(zz, 1 - c, high)):
            send(src, dst, s_raw_s.at[i, k], s_raw_r.at[i, k], sib)

    row8 = lax.broadcasted_iota(jnp.int32, (BLK, BLK), 0) // 8
    col8 = lax.broadcasted_iota(jnp.int32, (BLK, BLK), 1) // 8
    upper = row8 <= col8
    middle = row8 == col8

    def gram(zz, k):
        cols = pl.ds(pl.multiple_of(1024 * zz + BLK * k, BLK), BLK)
        tok = raw[:, cols]
        return lax.dot_general(tok, tok, (((0,), (0,)), ((), ())), preferred_element_type=F32)

    @pl.loop(0, NZ)
    def _(i):
        zz = (z + 1 + i) % NZ
        for k, (src, dst) in enumerate(local_parts(zz, c, low)):
            pltpu.make_async_copy(src, dst, s_loc.at[i, k]).wait()
        for k, (src, dst) in enumerate(local_parts(zz, c, high)):
            arrived(dst, s_raw_r.at[i, k])
        for xx in range(NX):
            first = gram(zz, 2 * xx)
            second = gram(zz, 2 * xx + 1)
            packed = jnp.where(upper, first, second).reshape(NY, 2, 8, BLK)
            extra = jnp.sum(jnp.where(middle, second, 0.0).reshape(16, 8, BLK), axis=0)
            ta[zz, xx, pl.ds(0, NY)] = packed[:, 0]
            ta[zz, xx, NY] = extra
            if xx < 2:
                tb[:, i, xx] = packed[:, 1]
            else:
                tg[zz, xx - 2] = packed[:, 1]
        for j in range(1, NX):
            to = (x + j) % NX
            send(ta.at[zz, to], ra.at[j - 1, zz], s_a.at[j - 1, i], r_a.at[j - 1, i], device(to, y, z, c))

        @pl.when(i < NZ - 1)
        def _():
            send(tg.at[zz], rg.at[i], s_g.at[i], r_g.at[i], device(x, y, zz, c))

        @pl.when(i % 4 == 3)
        def _():
            half = i // 4
            for j in range(1, NY):
                to = (y + j) % NY
                send(tb.at[to, pl.ds(4 * half, 4)], rb.at[j - 1, pl.ds(4 * half, 4)],
                     s_b.at[j - 1, half], r_b.at[j - 1, half], device(x, to, z, c))

    @pl.loop(0, NZ)
    def _(i):
        zz = (z + 1 + i) % NZ
        total = ta[zz, x]
        for j in range(NX - 1):
            arrived(ra.at[j, zz], r_a.at[j, i])
            total = total + ra[j, zz]
        a2[zz] = total

        @pl.when(i < NZ - 1)
        def _():
            send(a2.at[zz], ra2.at[i], s_a2.at[i], r_a2.at[i], device(x, y, zz, c))

    for j in range(NZ - 1):
        arrived(rg.at[j], r_g.at[j])
    for k in range(2):
        total = tg[z, k]
        for j in range(NZ - 1):
            total = total + rg[j, k]
        for yy in range(NY):
            g2[yy, k] = total[yy]
    for j in range(1, NY):
        to = (y + j) % NY
        send(g2.at[to], rg2.at[j - 1], s_g2.at[j - 1], r_g2.at[j - 1], device(x, to, z, c))

    for j in range(NY - 1):
        for half in range(2):
            arrived(rb.at[j, pl.ds(4 * half, 4)], r_b.at[j, half])

    @pl.loop(0, NZ)
    def _(i):
        total = tb[y, i]
        for j in range(NY - 1):
            total = total + rb[j, i]
        b2[i] = total
        zz = (z + 1 + i) % NZ

        @pl.when(i < NZ - 1)
        def _():
            send(b2.at[i], rb2.at[i], s_b2.at[i], r_b2.at[i], device(x, y, zz, c))

    total = a2[z]
    for j in range(NZ - 1):
        arrived(ra2.at[j], r_a2.at[j])
        total = total + ra2[j]
    for yy in range(NY):
        a3[yy, 0] = total[yy]
        a3[yy, 1] = total[NY]
    for j in range(1, NY):
        to = (y + j) % NY
        send(a3.at[to], ra3.at[j - 1], s_a3.at[j - 1], r_a3.at[j - 1], device(x, to, z, c))

    total = g2[y]
    for j in range(NY - 1):
        arrived(rg2.at[j], r_g2.at[j])
        total = total + rg2[j]
    x3[2] = total[0]
    x3[3] = total[1]
    total = b2[NZ - 1]
    for j in range(NZ - 1):
        arrived(rb2.at[j], r_b2.at[j])
        total = total + rb2[j]
    x3[0] = total[0]
    x3[1] = total[1]
    for j in range(1, NX):
        to = (x + j) % NX
        send(x3.at[to], rx3.at[j - 1], s_x3.at[j - 1], r_x3.at[j - 1], device(to, y, z, c))

    total = a3[y]
    for j in range(NY - 1):
        arrived(ra3.at[j], r_a3.at[j])
        total = total + ra3[j]
    fin[0] = total[0]
    d_out[...] = total[1]
    total = x3[x]
    for j in range(NX - 1):
        arrived(rx3.at[j], r_x3.at[j])
        total = total + rx3[j]
    fin[1] = total

    m_out[y] = fin[...]
    for j in range(1, NY):
        to = (y + j) % NY
        send(fin, m_out.at[y], s_f.at[j - 1], r_f.at[j - 1], device(x, to, z, c))
    for j in range(1, NY):
        arrived(m_out.at[(y - j + NY) % NY], r_f.at[j - 1])

    @pl.loop(0, NZ)
    def _(i):
        zz = (z + 1 + i) % NZ
        for k, (src, dst) in enumerate(local_parts(zz, 1 - c, high)):
            arrived(src, s_raw_s.at[i, k])
        for j in range(NX - 1):
            arrived(ta.at[zz, x], s_a.at[j, i])

    for j in range(NZ - 1):
        arrived(tg.at[j], s_g.at[j])
        arrived(a2.at[j], s_a2.at[j])
        arrived(b2.at[j], s_b2.at[j])
    for j in range(NY - 1):
        for half in range(2):
            arrived(tb.at[j, pl.ds(4 * half, 4)], s_b.at[j, half])
        arrived(g2.at[j], s_g2.at[j])
        arrived(a3.at[j], s_a3.at[j])
        arrived(fin, s_f.at[j])
    for j in range(NX - 1):
        arrived(x3.at[j], s_x3.at[j])


def gram_sums(hid, grd):
    dma = pltpu.SemaphoreType.DMA
    tile = (8, BLK)
    vm = pltpu.VMEM
    return pl.pallas_call(
        gram_kernel,
        out_shape=(jax.ShapeDtypeStruct((NY, 2) + tile, F32), jax.ShapeDtypeStruct(tile, F32)),
        in_specs=[pl.BlockSpec(memory_space=pl.ANY)] * 2,
        out_specs=[pl.BlockSpec(memory_space=pltpu.VMEM)] * 2,
        scratch_shapes=[
            vm((256, 8192), BF16),
            vm((NZ, NX, NY + 1) + tile, F32),
            vm((NY, NZ, 2) + tile, F32),
            vm((NZ, 2, NY) + tile, F32),
            vm((NX - 1, NZ, NY + 1) + tile, F32),
            vm((NY - 1, NZ, 2) + tile, F32),
            vm((NZ - 1, 2, NY) + tile, F32),
            vm((NZ, NY + 1) + tile, F32),
            vm((NZ, 2) + tile, F32),
            vm((NY, 2) + tile, F32),
            vm((NZ - 1, NY + 1) + tile, F32),
            vm((NZ - 1, 2) + tile, F32),
            vm((NY - 1, 2) + tile, F32),
            vm((NY, 2) + tile, F32),
            vm((NX,) + tile, F32),
            vm((NY - 1, 2) + tile, F32),
            vm((NX - 1,) + tile, F32),
            vm((2,) + tile, F32),
            dma((NZ, 2)), dma((NZ, 2)), dma((NZ, 2)),
            dma((NX - 1, NZ)), dma((NX - 1, NZ)),
            dma((NY - 1, 2)), dma((NY - 1, 2)),
            dma((NZ - 1,)), dma((NZ - 1,)),
            dma((NZ - 1,)), dma((NZ - 1,)),
            dma((NZ - 1,)), dma((NZ - 1,)),
            dma((NY - 1,)), dma((NY - 1,)),
            dma((NY - 1,)), dma((NY - 1,)),
            dma((NX - 1,)), dma((NX - 1,)),
            dma((NY - 1,)), dma((NY - 1,)),
        ],
        compiler_params=pltpu.CompilerParams(
            collective_id=0, has_side_effects=True, vmem_limit_bytes=40 * 2**20
        ),
        cost_estimate=pl.CostEstimate(flops=2 * 64 * 256 * BLK * BLK, bytes_accessed=4 * 2**20, transcendentals=0),
        name="gram_sums",
    )(hid, grd)


def split3(value):
    high = value.astype(BF16)
    rest = value - high.astype(F32)
    mid = rest.astype(BF16)
    return high, mid, (rest - mid.astype(F32)).astype(BF16)


def product(left, right):
    lh, lm, ll = split3(left)
    rh, rm, rl = split3(right)

    def dot(a, b):
        return jnp.dot(a, b, preferred_element_type=F32)

    small = dot(jnp.concatenate((lm, ll), axis=1), jnp.concatenate((rm, rh), axis=0))
    middle = dot(jnp.concatenate((lh, lm), axis=1), jnp.concatenate((rm, rh), axis=0))
    large = dot(jnp.concatenate((lh, lh), axis=1), jnp.concatenate((rh, rl), axis=0))
    return large + (middle + small)


def newton_kernel(token_total, m_ref, d_ref, x_ref):
    _, y, _, _ = place()
    second = (y // NYL) == 1
    packed = m_ref[...].reshape(BLK, BLK)
    extra = jnp.broadcast_to(d_ref[...][None], (16, 8, BLK)).reshape(BLK, BLK)
    row = lax.broadcasted_iota(jnp.int32, (BLK, BLK), 0)
    col = lax.broadcasted_iota(jnp.int32, (BLK, BLK), 1)
    turned = packed.T
    first_block = jnp.where(row // 8 <= col // 8, packed, turned)
    second_block = jnp.where(row // 8 == col // 8, extra, jnp.where(row // 8 > col // 8, packed, turned))
    sums = jnp.where(second, second_block, first_block)
    identity = jnp.where(row == col, 1.0, 0.0)
    factor = sums / token_total + DAMPING * identity
    bound = jnp.max(jnp.sum(jnp.abs(factor), axis=1, keepdims=True), axis=0, keepdims=True)
    both = jnp.concatenate((factor / bound, identity / bound), axis=1)

    def refine(step, both):
        return 2.0 * both - product(both[:, :BLK], both)

    both = lax.fori_loop(0, ITERS, refine, both)
    x_ref[...] = both[:, BLK:].astype(BF16)


def newton(token_total, packed, extra):
    return pl.pallas_call(
        lambda *refs: newton_kernel(token_total, *refs),
        out_shape=jax.ShapeDtypeStruct((BLK, BLK), BF16),
        in_specs=[pl.BlockSpec(memory_space=pltpu.VMEM)] * 2,
        out_specs=pl.BlockSpec(memory_space=pltpu.VMEM),
        cost_estimate=pl.CostEstimate(flops=2 * 14 * 6 * 2 * BLK**3, bytes_accessed=2**17, transcendentals=0),
        name="newton",
    )(packed, extra)


def spread_kernel(inv, owner_a, owner_g, r4, r5,
                  p0, kept, s4, s_0, r_0, s_z, r_z, s_k, r_k, s_4, r_4, s_5, r_5):
    x, y, z, c = place()
    yh, yl = y // NYL, y % NYL
    dp, own = lax.axis_index("dp"), lax.axis_index("own")
    e = 2 * x + yh
    sib = device(x, y, z, 1 - c)

    def peer(j):
        other = (e + j) % 8
        return other, device(other // 2, (other % 2) * NYL + yl, z, c)

    barrier = pltpu.get_barrier_semaphore()
    pl.semaphore_signal(barrier, inc=1, device_id=sib, device_id_type=MESH)
    for j in range(1, 8):
        pl.semaphore_signal(barrier, inc=1, device_id=peer(j)[1], device_id_type=MESH)
    for j in range(1, NZ):
        pl.semaphore_signal(barrier, inc=1, device_id=device(x, y, (z + j) % NZ, c), device_id_type=MESH)

    def find_a(b, found):
        at = owner_a[b] - 3 * own
        return tuple(jnp.where(at == k, b, found[k]) for k in range(3))

    def find_g(b, found):
        return jnp.where(owner_g[b] == own, b, found)

    zero = jnp.int32(0)
    slot_a = lax.fori_loop(0, 96, find_a, (zero, zero, zero))
    slot_g = lax.fori_loop(0, 32, find_g, zero)

    def at_a(b):
        return b // 48, (b % 48) // 6, b % 6

    def at_g(b):
        return b // 16, (b % 16) // 2, 6 + b % 2

    want = [tuple(jnp.where(c == 0, s, n) for s, n in zip(at_a(slot_a[k]), at_a(3 * own + k))) for k in range(3)]
    want.append(at_g(slot_g))

    pl.semaphore_wait(barrier, 1 + 7 + (NZ - 1))

    for j in range(1, 8):
        other, to = peer(j)
        send(inv.at[pl.ds(pl.multiple_of(16 * other, 16), 16)], p0.at[e], s_0.at[j - 1], r_0.at[j - 1], to)
    p0[e] = inv[pl.ds(pl.multiple_of(16 * e, 16), 16), :]
    for j in range(1, 8):
        arrived(p0.at[(e - j + 8) % 8], r_0.at[j - 1])
    for j in range(1, NZ):
        send(p0, kept.at[c, z], s_z.at[j - 1], r_z.at[j - 1], device(x, y, (z + j) % NZ, c))
    send(p0, kept.at[c, z], s_k.at[0], r_k.at[0], sib)
    kept[c, z] = p0[...]
    for j in range(1, NZ):
        zz = (z - j + NZ) % NZ
        arrived(kept.at[c, zz], r_z.at[j - 1])
        send(kept.at[c, zz], kept.at[c, zz], s_k.at[j], r_k.at[j], sib)
    for j in range(NZ):
        arrived(kept.at[1 - c, (z - j + NZ) % NZ], r_k.at[j])

    shared = [kept[w] for w in want]
    for j in range(1, 9):
        other, to = peer(j)
        for k in range(4):
            s4[other, k] = shared[k]
        for k in range(2):
            s4[other, 4 + k] = kept[at_g(2 * (2 * other + c) + k)]
        if j < 8:
            send(s4.at[other], r4.at[e], s_4.at[j - 1], r_4.at[j - 1], to)
    r4[e] = s4[e]
    send(s4.at[e, pl.ds(0, 4)], r5.at[e], s_5.at[0], r_5.at[0], sib)
    for j in range(1, 8):
        other = (e - j + 8) % 8
        arrived(r4.at[other], r_4.at[j - 1])
        send(r4.at[other, pl.ds(0, 4)], r5.at[other], s_5.at[j], r_5.at[j], sib)
    for j in range(8):
        arrived(r5.at[(e - j + 8) % 8], r_5.at[j])

    for j in range(7):
        arrived(p0.at[0], s_0.at[j])
        arrived(p0, s_z.at[j])
        arrived(s4.at[0], s_4.at[j])
    for j in range(8):
        arrived(p0, s_k.at[j])
        arrived(r5.at[0], s_5.at[j])


def spread(inv, owner_a, owner_g):
    dma = pltpu.SemaphoreType.DMA
    vm = pltpu.VMEM
    piece = (16, BLK)
    return pl.pallas_call(
        spread_kernel,
        out_shape=(jax.ShapeDtypeStruct((8, 6) + piece, BF16), jax.ShapeDtypeStruct((8, 4) + piece, BF16)),
        in_specs=[pl.BlockSpec(memory_space=pltpu.VMEM)] + [pl.BlockSpec(memory_space=pltpu.SMEM)] * 2,
        out_specs=[pl.BlockSpec(memory_space=pltpu.VMEM)] * 2,
        scratch_shapes=[
            vm((8,) + piece, BF16), vm((2, NZ, 8) + piece, BF16), vm((8, 6) + piece, BF16),
            dma((7,)), dma((7,)), dma((7,)), dma((7,)), dma((8,)), dma((8,)),
            dma((7,)), dma((7,)), dma((8,)), dma((8,)),
        ],
        compiler_params=pltpu.CompilerParams(
            collective_id=1, has_side_effects=True, vmem_limit_bytes=16 * 2**20
        ),
        name="spread_inverses",
    )(inv, owner_a, owner_g)


def apply_kernel(r4, r5, w, a_out, g_out, p_out):
    _, _, _, c = place()

    def whole(ref, k):
        return ref[:, k].reshape(BLK, BLK)

    mine = [whole(r4, k) for k in range(6)]
    theirs = [whole(r5, k) for k in range(4)]
    even = c == 0
    for k in range(3):
        a_out[k] = jnp.where(even, mine[k], theirs[k])
    g_out[0] = mine[3]
    for k in range(3):
        nat = jnp.where(even, theirs[k], mine[k])
        rows = pl.ds(BLK * k, BLK)
        left = jnp.dot(nat, w[rows, :], preferred_element_type=F32).astype(BF16)
        for m in range(2):
            cols = slice(BLK * m, BLK * (m + 1))
            p_out[rows, cols] = jnp.dot(left[:, cols], mine[4 + m], preferred_element_type=F32)


def apply_inverses(r4, r5, w):
    return pl.pallas_call(
        apply_kernel,
        out_shape=(
            jax.ShapeDtypeStruct((3, BLK, BLK), BF16),
            jax.ShapeDtypeStruct((1, BLK, BLK), BF16),
            jax.ShapeDtypeStruct(w.shape, F32),
        ),
        name="apply_inverses",
    )(r4, r5, w)


def on_device(hidden_act, out_grad, weight_grad, owner_a, owner_g):
    token_total = hidden_act.shape[0] * lax.axis_size("own") * lax.axis_size("dp")
    packed, extra = gram_sums(hidden_act, out_grad)
    inverse = newton(token_total, packed, extra)
    r4, r5 = spread(inverse, owner_a, owner_g)
    return apply_inverses(r4, r5, weight_grad)


def solution(mesh):
    placed = (P(("dp", "own"), None), P(("dp", "own"), None), P("own", "dp"), P(), P())
    return jax.shard_map(
        on_device,
        mesh=mesh,
        in_specs=placed,
        out_specs=(P("own", None, None), P("own", None, None), P("own", "dp")),
        check_vma=False,
    )
```

```python
import jax
import jax.numpy as jnp
from jax import lax
from jax.experimental import pallas as pl
from jax.experimental.pallas import tpu as pltpu
from jax.sharding import PartitionSpec as P

BLK = 128
ITERS = 14
DAMPING = 0.05
NX, NY, NZ, NYL = 4, 8, 8, 4
MESH = pl.DeviceIdType.MESH
F32 = jnp.float32
BF16 = jnp.bfloat16


def place():
    dp = lax.axis_index("dp")
    own = lax.axis_index("own")
    return dp // 4, ((dp // 2) % 2) * NYL + own % NYL, own // NYL, dp % 2


def device(x, y, z, c):
    return (x * 4 + (y // NYL) * 2 + c, z * NYL + y % NYL)


def send(src, dst, send_sem, recv_sem, to):
    copy = pltpu.make_async_remote_copy(
        src_ref=src, dst_ref=dst, send_sem=send_sem, recv_sem=recv_sem,
        device_id=to, device_id_type=MESH,
    )
    copy.start()


def arrived(ref, sem):
    pltpu.make_async_copy(ref, ref, sem).wait()


def gram_kernel(hid, grd, m_out, d_out,
                raw, ta, tb, tg, ra, rb, rg, a2, b2, g2, ra2, rb2, rg2, a3, x3, ra3, rx3, fin,
                s_loc, s_raw_s, s_raw_r, s_a, r_a, s_b, r_b, s_g, r_g,
                s_a2, r_a2, s_b2, r_b2, s_g2, r_g2, s_a3, r_a3, s_x3, r_x3, s_f, r_f):
    x, y, z, c = place()
    sib = device(x, y, z, 1 - c)

    barrier = pltpu.get_barrier_semaphore()
    pl.semaphore_signal(barrier, inc=1, device_id=sib, device_id_type=MESH)
    for j in range(1, NX):
        pl.semaphore_signal(barrier, inc=1, device_id=device((x + j) % NX, y, z, c), device_id_type=MESH)
    for j in range(1, NY):
        pl.semaphore_signal(barrier, inc=1, device_id=device(x, (y + j) % NY, z, c), device_id_type=MESH)
    for j in range(1, NZ):
        pl.semaphore_signal(barrier, inc=1, device_id=device(x, y, (z + j) % NZ, c), device_id_type=MESH)

    def local_parts(zz, core, rows):
        return (
            (hid.at[:, pl.ds(pl.multiple_of(6144 * core + 768 * zz, 128), 768)],
             raw.at[rows, pl.ds(pl.multiple_of(1024 * zz, 128), 768)]),
            (grd.at[:, pl.ds(pl.multiple_of(2048 * core + 256 * zz, 128), 256)],
             raw.at[rows, pl.ds(pl.multiple_of(1024 * zz + 768, 128), 256)]),
        )

    low, high = pl.ds(0, 128), pl.ds(128, 128)

    @pl.loop(0, NZ)
    def _(i):
        zz = (z + 1 + i) % NZ
        for k, (src, dst) in enumerate(local_parts(zz, c, low)):
            pltpu.make_async_copy(src, dst, s_loc.at[i, k]).start()

    pl.semaphore_wait(barrier, 1 + (NX - 1) + (NY - 1) + (NZ - 1))

    @pl.loop(0, NZ)
    def _(i):
        zz = (z + 1 + i) % NZ
        for k, (src, dst) in enumerate(local_parts(zz, 1 - c, high)):
            send(src, dst, s_raw_s.at[i, k], s_raw_r.at[i, k], sib)

    row8 = lax.broadcasted_iota(jnp.int32, (BLK, BLK), 0) // 8
    col8 = lax.broadcasted_iota(jnp.int32, (BLK, BLK), 1) // 8
    upper = row8 <= col8
    middle = row8 == col8

    def gram(zz, k):
        cols = pl.ds(pl.multiple_of(1024 * zz + BLK * k, BLK), BLK)
        tok = raw[:, cols]
        return lax.dot_general(tok, tok, (((0,), (0,)), ((), ())), preferred_element_type=F32)

    @pl.loop(0, NZ)
    def _(i):
        zz = (z + 1 + i) % NZ
        for k, (src, dst) in enumerate(local_parts(zz, c, low)):
            pltpu.make_async_copy(src, dst, s_loc.at[i, k]).wait()
        for k, (src, dst) in enumerate(local_parts(zz, c, high)):
            arrived(dst, s_raw_r.at[i, k])
        for xx in range(NX):
            first = gram(zz, 2 * xx)
            second = gram(zz, 2 * xx + 1)
            packed = jnp.where(upper, first, second).reshape(NY, 2, 8, BLK)
            extra = jnp.sum(jnp.where(middle, second, 0.0).reshape(16, 8, BLK), axis=0)
            ta[zz, xx, pl.ds(0, NY)] = packed[:, 0]
            ta[zz, xx, NY] = extra
            if xx < 2:
                tb[:, i, xx] = packed[:, 1]
            else:
                tg[zz, xx - 2] = packed[:, 1]
        for j in range(1, NX):
            to = (x + j) % NX
            send(ta.at[zz, to], ra.at[j - 1, zz], s_a.at[j - 1, i], r_a.at[j - 1, i], device(to, y, z, c))

        @pl.when(i < NZ - 1)
        def _():
            send(tg.at[zz], rg.at[i], s_g.at[i], r_g.at[i], device(x, y, zz, c))

        @pl.when(i % 4 == 3)
        def _():
            half = i // 4
            for j in range(1, NY):
                to = (y + j) % NY
                send(tb.at[to, pl.ds(4 * half, 4)], rb.at[j - 1, pl.ds(4 * half, 4)],
                     s_b.at[j - 1, half], r_b.at[j - 1, half], device(x, to, z, c))

    @pl.loop(0, NZ)
    def _(i):
        zz = (z + 1 + i) % NZ
        total = ta[zz, x]
        for j in range(NX - 1):
            arrived(ra.at[j, zz], r_a.at[j, i])
            total = total + ra[j, zz]
        a2[zz] = total

        @pl.when(i < NZ - 1)
        def _():
            send(a2.at[zz], ra2.at[i], s_a2.at[i], r_a2.at[i], device(x, y, zz, c))

    for j in range(NZ - 1):
        arrived(rg.at[j], r_g.at[j])
    for k in range(2):
        total = tg[z, k]
        for j in range(NZ - 1):
            total = total + rg[j, k]
        for yy in range(NY):
            g2[yy, k] = total[yy]
    for j in range(1, NY):
        to = (y + j) % NY
        send(g2.at[to], rg2.at[j - 1], s_g2.at[j - 1], r_g2.at[j - 1], device(x, to, z, c))

    for j in range(NY - 1):
        for half in range(2):
            arrived(rb.at[j, pl.ds(4 * half, 4)], r_b.at[j, half])

    @pl.loop(0, NZ)
    def _(i):
        total = tb[y, i]
        for j in range(NY - 1):
            total = total + rb[j, i]
        b2[i] = total
        zz = (z + 1 + i) % NZ

        @pl.when(i < NZ - 1)
        def _():
            send(b2.at[i], rb2.at[i], s_b2.at[i], r_b2.at[i], device(x, y, zz, c))

    total = a2[z]
    for j in range(NZ - 1):
        arrived(ra2.at[j], r_a2.at[j])
        total = total + ra2[j]
    for yy in range(NY):
        a3[yy, 0] = total[yy]
        a3[yy, 1] = total[NY]
    for j in range(1, NY):
        to = (y + j) % NY
        send(a3.at[to], ra3.at[j - 1], s_a3.at[j - 1], r_a3.at[j - 1], device(x, to, z, c))

    total = g2[y]
    for j in range(NY - 1):
        arrived(rg2.at[j], r_g2.at[j])
        total = total + rg2[j]
    x3[2] = total[0]
    x3[3] = total[1]
    total = b2[NZ - 1]
    for j in range(NZ - 1):
        arrived(rb2.at[j], r_b2.at[j])
        total = total + rb2[j]
    x3[0] = total[0]
    x3[1] = total[1]
    for j in range(1, NX):
        to = (x + j) % NX
        send(x3.at[to], rx3.at[j - 1], s_x3.at[j - 1], r_x3.at[j - 1], device(to, y, z, c))

    total = a3[y]
    for j in range(NY - 1):
        arrived(ra3.at[j], r_a3.at[j])
        total = total + ra3[j]
    fin[0] = total[0]
    d_out[...] = total[1]
    total = x3[x]
    for j in range(NX - 1):
        arrived(rx3.at[j], r_x3.at[j])
        total = total + rx3[j]
    fin[1] = total

    m_out[y] = fin[...]
    for j in range(1, NY):
        to = (y + j) % NY
        send(fin, m_out.at[y], s_f.at[j - 1], r_f.at[j - 1], device(x, to, z, c))
    for j in range(1, NY):
        arrived(m_out.at[(y - j + NY) % NY], r_f.at[j - 1])

    @pl.loop(0, NZ)
    def _(i):
        zz = (z + 1 + i) % NZ
        for k, (src, dst) in enumerate(local_parts(zz, 1 - c, high)):
            arrived(src, s_raw_s.at[i, k])
        for j in range(NX - 1):
            arrived(ta.at[zz, x], s_a.at[j, i])

    for j in range(NZ - 1):
        arrived(tg.at[j], s_g.at[j])
        arrived(a2.at[j], s_a2.at[j])
        arrived(b2.at[j], s_b2.at[j])
    for j in range(NY - 1):
        for half in range(2):
            arrived(tb.at[j, pl.ds(4 * half, 4)], s_b.at[j, half])
        arrived(g2.at[j], s_g2.at[j])
        arrived(a3.at[j], s_a3.at[j])
        arrived(fin, s_f.at[j])
    for j in range(NX - 1):
        arrived(x3.at[j], s_x3.at[j])


def gram_sums(hid, grd):
    dma = pltpu.SemaphoreType.DMA
    tile = (8, BLK)
    vm = pltpu.VMEM
    return pl.pallas_call(
        gram_kernel,
        out_shape=(jax.ShapeDtypeStruct((NY, 2) + tile, F32), jax.ShapeDtypeStruct(tile, F32)),
        in_specs=[pl.BlockSpec(memory_space=pl.ANY)] * 2,
        out_specs=[pl.BlockSpec(memory_space=pltpu.VMEM)] * 2,
        scratch_shapes=[
            vm((256, 8192), BF16),
            vm((NZ, NX, NY + 1) + tile, F32),
            vm((NY, NZ, 2) + tile, F32),
            vm((NZ, 2, NY) + tile, F32),
            vm((NX - 1, NZ, NY + 1) + tile, F32),
            vm((NY - 1, NZ, 2) + tile, F32),
            vm((NZ - 1, 2, NY) + tile, F32),
            vm((NZ, NY + 1) + tile, F32),
            vm((NZ, 2) + tile, F32),
            vm((NY, 2) + tile, F32),
            vm((NZ - 1, NY + 1) + tile, F32),
            vm((NZ - 1, 2) + tile, F32),
            vm((NY - 1, 2) + tile, F32),
            vm((NY, 2) + tile, F32),
            vm((NX,) + tile, F32),
            vm((NY - 1, 2) + tile, F32),
            vm((NX - 1,) + tile, F32),
            vm((2,) + tile, F32),
            dma((NZ, 2)), dma((NZ, 2)), dma((NZ, 2)),
            dma((NX - 1, NZ)), dma((NX - 1, NZ)),
            dma((NY - 1, 2)), dma((NY - 1, 2)),
            dma((NZ - 1,)), dma((NZ - 1,)),
            dma((NZ - 1,)), dma((NZ - 1,)),
            dma((NZ - 1,)), dma((NZ - 1,)),
            dma((NY - 1,)), dma((NY - 1,)),
            dma((NY - 1,)), dma((NY - 1,)),
            dma((NX - 1,)), dma((NX - 1,)),
            dma((NY - 1,)), dma((NY - 1,)),
        ],
        compiler_params=pltpu.CompilerParams(
            collective_id=0, has_side_effects=True, vmem_limit_bytes=62 * 2**20
        ),
        cost_estimate=pl.CostEstimate(flops=2 * 64 * 256 * BLK * BLK, bytes_accessed=4 * 2**20, transcendentals=0),
        name="gram_sums",
    )(hid, grd)


def split3(value):
    high = value.astype(BF16)
    rest = value - high.astype(F32)
    mid = rest.astype(BF16)
    return high, mid, (rest - mid.astype(F32)).astype(BF16)


def product(left, right):
    lh, lm, ll = split3(left)
    rh, rm, rl = split3(right)

    def dot(a, b):
        return jnp.dot(a, b, preferred_element_type=F32)

    small = dot(jnp.concatenate((lm, ll), axis=1), jnp.concatenate((rm, rh), axis=0))
    middle = dot(jnp.concatenate((lh, lm), axis=1), jnp.concatenate((rm, rh), axis=0))
    large = dot(jnp.concatenate((lh, lh), axis=1), jnp.concatenate((rh, rl), axis=0))
    return large + (middle + small)


def newton_kernel(token_total, m_hbm, d_hbm, x_hbm, m_ref, d_ref, x_ref, sem):
    loads = [pltpu.make_async_copy(m_hbm, m_ref, sem.at[0]), pltpu.make_async_copy(d_hbm, d_ref, sem.at[1])]
    for load in loads:
        load.start()
    for load in loads:
        load.wait()
    _, y, _, _ = place()
    second = (y % 2) == 1
    packed = m_ref[...].reshape(BLK, BLK)
    extra = jnp.broadcast_to(d_ref[...][None], (16, 8, BLK)).reshape(BLK, BLK)
    row = lax.broadcasted_iota(jnp.int32, (BLK, BLK), 0)
    col = lax.broadcasted_iota(jnp.int32, (BLK, BLK), 1)
    turned = packed.T
    first_block = jnp.where(row // 8 <= col // 8, packed, turned)
    second_block = jnp.where(row // 8 == col // 8, extra, jnp.where(row // 8 > col // 8, packed, turned))
    sums = jnp.where(second, second_block, first_block)
    identity = jnp.where(row == col, 1.0, 0.0)
    factor = sums / token_total + DAMPING * identity
    bound = jnp.max(jnp.sum(jnp.abs(factor), axis=1, keepdims=True), axis=0, keepdims=True)
    both = jnp.concatenate((factor / bound, identity / bound), axis=1)

    def refine(step, both):
        return 2.0 * both - product(both[:, :BLK], both)

    both = lax.fori_loop(0, ITERS, refine, both)
    x_ref[...] = both[:, BLK:].astype(BF16)
    store = pltpu.make_async_copy(x_ref, x_hbm, sem.at[0])
    store.start()
    store.wait()


def newton(token_total, packed, extra):
    out = jax.ShapeDtypeStruct((BLK, BLK), BF16)
    return pl.pallas_call(
        lambda *refs: newton_kernel(token_total, *refs),
        out_shape=out,
        in_specs=[pl.BlockSpec(memory_space=pl.ANY)] * 2,
        out_specs=pl.BlockSpec(memory_space=pl.ANY),
        scratch_shapes=[pltpu.VMEM(a.shape, a.dtype) for a in (packed, extra, out)] + [pltpu.SemaphoreType.DMA((2,))],
        compiler_params=pltpu.CompilerParams(vmem_limit_bytes=62 * 2**20),
        name="newton",
    )(packed, extra)


def spread_kernel(inv, owner_a, owner_g, r4, r5,
                  kept, es, er, s4, s_l, s_p, r_p, s_z, r_z, s_q, r_q, s_e, r_e, s_4, r_4, s_5, r_5):
    x, y, z, c = place()
    own = lax.axis_index("own")
    yh, q = y // NYL, y % 2
    sib = device(x, y, z, 1 - c)

    barrier = pltpu.get_barrier_semaphore()
    pl.semaphore_signal(barrier, inc=1, device_id=sib, device_id_type=MESH)
    for j in range(1, NX):
        pl.semaphore_signal(barrier, inc=1, device_id=device((x + j) % NX, y, z, c), device_id_type=MESH)
    for step in (1, NY - 1):
        pl.semaphore_signal(barrier, inc=1, device_id=device(x, (y + step) % NY, z, c), device_id_type=MESH)
    for j in range(1, NZ):
        pl.semaphore_signal(barrier, inc=1, device_id=device(x, y, (z + j) % NZ, c), device_id_type=MESH)

    mine_here = pltpu.make_async_copy(inv.at[pl.ds(pl.multiple_of(32 * x, 32), 32)], kept.at[q, z, x], s_l)
    mine_here.start()

    def find_a(b, found):
        at = owner_a[b] - 3 * own
        return tuple(jnp.where(at == k, b, found[k]) for k in range(3))

    def find_g(b, found):
        return jnp.where(owner_g[b] == own, b, found)

    zero = jnp.int32(0)
    slot_a = lax.fori_loop(0, 96, find_a, (zero, zero, zero))
    slot_g = lax.fori_loop(0, 32, find_g, zero)

    def at_a(b):
        return b % 2, (b % 48) // 6, (b % 6) // 2

    def at_g(b):
        return b % 2, (b % 16) // 2, 3

    def entry(core, k):
        if k == 3:
            return slot_g // 16, at_g(slot_g)
        block = jnp.where(core == 0, slot_a[k], 3 * own + k)
        return block // 48, at_a(block)

    mine = [entry(c, k) for k in range(4)]
    theirs = [entry(1 - c, k) for k in range(4)]
    mine_here.wait()
    pl.semaphore_wait(barrier, 1 + (NX - 1) + 2 + (NZ - 1))

    for j in range(1, NX):
        to = (x + j) % NX
        send(inv.at[pl.ds(pl.multiple_of(32 * to, 32), 32)], kept.at[q, z, x],
             s_p.at[j - 1], r_p.at[j - 1], device(to, y, z, c))
    for j in range(1, NX):
        arrived(kept.at[q, z, (x - j + NX) % NX], r_p.at[j - 1])
    for j in range(1, NZ):
        send(kept.at[q, z], kept.at[q, z], s_z.at[j - 1], r_z.at[j - 1], device(x, y, (z + j) % NZ, c))

    def to_neighbours(zz, j):
        for k, step in enumerate((1, NY - 1)):
            half = kept.at[q, zz, pl.ds(2 * k, 2)]
            send(half, half, s_q.at[j, k], r_q.at[j, k], device(x, (y + step) % NY, z, c))

    to_neighbours(z, 0)
    for j in range(1, NZ):
        zz = (z - j + NZ) % NZ
        arrived(kept.at[q, zz], r_z.at[j - 1])
        to_neighbours(zz, j)
    for j in range(NZ):
        zz = (z - j + NZ) % NZ
        for k in range(2):
            arrived(kept.at[1 - q, zz, pl.ds(2 * k, 2)], r_q.at[j, k])

    for k in range(4):
        es[k] = kept[theirs[k][1]]
    for m in range(2):
        for k in range(2):
            es[4 + 2 * m + k] = kept[at_g(8 * (2 * c + m) + 4 * yh + 2 * (1 - c) + k)]
    send(es, er, s_e.at[0], r_e.at[0], sib)
    values = [kept[mine[k][1]] for k in range(4)]
    arrived(er, r_e.at[0])
    values = [jnp.where(mine[k][0] == c, values[k], er[k]) for k in range(4)]
    for j in range(1, NX + 1):
        to = (x + j) % NX
        for k in range(4):
            s4[to, k] = values[k]
        for k in range(2):
            here = kept[at_g(8 * to + 4 * yh + 2 * c + k)]
            s4[to, 4 + k] = jnp.where(to // 2 == c, here, er[4 + 2 * (to % 2) + k])
        if j < NX:
            send(s4.at[to], r4.at[x], s_4.at[j - 1], r_4.at[j - 1], device(to, y, z, c))
    r4[x] = s4[x]
    send(s4.at[x, pl.ds(0, 4)], r5.at[x], s_5.at[0], r_5.at[0], sib)
    for j in range(1, NX):
        frm = (x - j + NX) % NX
        arrived(r4.at[frm], r_4.at[j - 1])
        send(r4.at[frm, pl.ds(0, 4)], r5.at[frm], s_5.at[j], r_5.at[j], sib)
    for j in range(NX):
        arrived(r5.at[(x - j + NX) % NX], r_5.at[j])

    for j in range(NZ):
        for k in range(2):
            arrived(kept.at[q, j, pl.ds(2 * k, 2)], s_q.at[j, k])
    for j in range(NZ - 1):
        arrived(kept.at[q, z], s_z.at[j])
    for j in range(NX - 1):
        arrived(kept.at[q, z, x], s_p.at[j])
        arrived(s4.at[j], s_4.at[j])
    arrived(es, s_e.at[0])
    for j in range(NX):
        arrived(r5.at[j], s_5.at[j])


def spread(inv, owner_a, owner_g):
    dma = pltpu.SemaphoreType.DMA
    vm = pltpu.VMEM
    piece = (32, BLK)
    shapes = ((NX - 1,), (NZ - 1,), (NZ, 2), (1,), (NX - 1,), (NX,))
    return pl.pallas_call(
        spread_kernel,
        out_shape=(jax.ShapeDtypeStruct((NX, 6) + piece, BF16), jax.ShapeDtypeStruct((NX, 4) + piece, BF16)),
        in_specs=[pl.BlockSpec(memory_space=pl.ANY)] + [pl.BlockSpec(memory_space=pltpu.SMEM)] * 2,
        out_specs=[pl.BlockSpec(memory_space=pltpu.VMEM)] * 2,
        scratch_shapes=[
            vm((2, NZ, NX) + piece, BF16), vm((8,) + piece, BF16), vm((8,) + piece, BF16), vm((NX, 6) + piece, BF16), dma,
        ] + [dma(shape) for shape in shapes for _ in range(2)],
        compiler_params=pltpu.CompilerParams(
            collective_id=1, has_side_effects=True, vmem_limit_bytes=62 * 2**20
        ),
        name="spread_inverses",
    )(inv, owner_a, owner_g)


def apply_kernel(r4_hbm, r5_hbm, w_hbm, a_hbm, g_hbm, p_hbm, r4, r5, w, a_out, g_out, p_out, s_in, s_out):
    _, _, _, c = place()
    loads = [
        pltpu.make_async_copy(src, dst, s_in.at[k])
        for k, (src, dst) in enumerate(((r4_hbm, r4), (r5_hbm, r5), (w_hbm, w)))
    ]
    for load in loads:
        load.start()
    for load in loads:
        load.wait()

    def whole(ref, k):
        return ref[:, k].reshape(BLK, BLK)

    mine = [whole(r4, k) for k in range(6)]
    theirs = [whole(r5, k) for k in range(4)]
    core0 = c == 0
    stores = []

    def store(src, dst):
        stores.append(pltpu.make_async_copy(src, dst, s_out.at[len(stores)]))
        stores[-1].start()

    for k in range(3):
        placed = jnp.where(core0, theirs[k], mine[k])
        rows = pl.ds(BLK * k, BLK)
        left = jnp.dot(placed, w[rows, :], preferred_element_type=F32).astype(BF16)
        for m in range(2):
            cols = slice(BLK * m, BLK * (m + 1))
            p_out[rows, cols] = jnp.dot(left[:, cols], mine[4 + m], preferred_element_type=F32)
        store(p_out.at[rows], p_hbm.at[rows])
    for k in range(3):
        a_out[k] = jnp.where(core0, mine[k], theirs[k])
    store(a_out, a_hbm)
    g_out[0] = mine[3]
    store(g_out, g_hbm)
    for each in stores:
        each.wait()


def apply_inverses(r4, r5, w):
    outs = (
        jax.ShapeDtypeStruct((3, BLK, BLK), BF16),
        jax.ShapeDtypeStruct((1, BLK, BLK), BF16),
        jax.ShapeDtypeStruct(w.shape, F32),
    )
    return pl.pallas_call(
        apply_kernel,
        out_shape=outs,
        in_specs=[pl.BlockSpec(memory_space=pl.ANY)] * 3,
        out_specs=[pl.BlockSpec(memory_space=pl.ANY)] * 3,
        scratch_shapes=[pltpu.VMEM(a.shape, a.dtype) for a in (r4, r5, w) + outs]
        + [pltpu.SemaphoreType.DMA((3,)), pltpu.SemaphoreType.DMA((5,))],
        compiler_params=pltpu.CompilerParams(vmem_limit_bytes=62 * 2**20),
        name="apply_inverses",
    )(r4, r5, w)


def on_device(hidden_act, out_grad, weight_grad, owner_a, owner_g):
    token_total = hidden_act.shape[0] * lax.axis_size("own") * lax.axis_size("dp")
    packed, extra = gram_sums(hidden_act, out_grad)
    inverse = newton(token_total, packed, extra)
    r4, r5 = spread(inverse, owner_a, owner_g)
    return apply_inverses(r4, r5, weight_grad)


def solution(mesh):
    placed = (P(("dp", "own"), None), P(("dp", "own"), None), P("own", "dp"), P(), P())
    return jax.shard_map(
        on_device,
        mesh=mesh,
        in_specs=placed,
        out_specs=(P("own", None, None), P("own", None, None), P("own", "dp")),
        check_vma=False,
    )
```

```python
import jax
import jax.numpy as jnp
from jax import lax
from jax.experimental import pallas as pl
from jax.experimental.pallas import tpu as pltpu
from jax.sharding import PartitionSpec as P

BLK = 128
ITERS = 14
FINE = 4
DAMPING = 0.05
NX, NY, NZ, NYL = 4, 8, 8, 4
MESH = pl.DeviceIdType.MESH
F32 = jnp.float32
BF16 = jnp.bfloat16


def place():
    dp = lax.axis_index("dp")
    own = lax.axis_index("own")
    return dp // 4, ((dp // 2) % 2) * NYL + own % NYL, own // NYL, dp % 2


def device(x, y, z, c):
    return (x * 4 + (y // NYL) * 2 + c, z * NYL + y % NYL)


def send(src, dst, send_sem, recv_sem, to):
    copy = pltpu.make_async_remote_copy(
        src_ref=src, dst_ref=dst, send_sem=send_sem, recv_sem=recv_sem,
        device_id=to, device_id_type=MESH,
    )
    copy.start()


def arrived(ref, sem):
    pltpu.make_async_copy(ref, ref, sem).wait()


def gram_kernel(hid, grd, m_out, d_out,
                raw, ta, tg, ra, rz, rg, rx, a3, r3, fin,
                s_loc, s_raw_s, s_raw_r, s_a, r_a, s_z, r_z, s_g, r_g, s_x, r_x, s_3, r_3, s_f, r_f):
    x, y, z, c = place()
    sib = device(x, y, z, 1 - c)

    barrier = pltpu.get_barrier_semaphore()
    pl.semaphore_signal(barrier, inc=1, device_id=sib, device_id_type=MESH)
    for j in range(1, NX):
        pl.semaphore_signal(barrier, inc=1, device_id=device((x + j) % NX, y, z, c), device_id_type=MESH)
    for j in range(1, NY):
        pl.semaphore_signal(barrier, inc=1, device_id=device(x, (y + j) % NY, z, c), device_id_type=MESH)
    for j in (1, NZ - 1):
        pl.semaphore_signal(barrier, inc=1, device_id=device(x, y, (z + j) % NZ, c), device_id_type=MESH)

    def target(i):
        return (z + 4 + (2 * (i % 2) - 1) * ((i + 1) // 2)) % NZ

    def onward(i):
        return device(x, y, (z + NZ + 1 - 2 * (i % 2)) % NZ, c)

    def parts(zz, core, rows):
        return (
            (hid.at[:, pl.ds(pl.multiple_of(6144 * core + 768 * zz, 128), 768)],
             raw.at[rows, pl.ds(pl.multiple_of(1024 * zz, 128), 768)]),
            (grd.at[:, pl.ds(pl.multiple_of(2048 * core + 256 * zz, 128), 256)],
             raw.at[rows, pl.ds(pl.multiple_of(1024 * zz + 768, 128), 256)]),
        )

    low, high = pl.ds(0, 128), pl.ds(128, 128)

    @pl.loop(0, NZ)
    def _(i):
        for k, (src, dst) in enumerate(parts(target(i), c, low)):
            pltpu.make_async_copy(src, dst, s_loc.at[i, k]).start()

    pl.semaphore_wait(barrier, 1 + (NX - 1) + (NY - 1) + 2)

    @pl.loop(0, NZ)
    def _(i):
        for k, (src, dst) in enumerate(parts(target(i), 1 - c, high)):
            send(src, dst, s_raw_s.at[i, k], s_raw_r.at[i, k], sib)

    row8 = lax.broadcasted_iota(jnp.int32, (BLK, BLK), 0) // 8
    col8 = lax.broadcasted_iota(jnp.int32, (BLK, BLK), 1) // 8
    upper = row8 <= col8
    middle = row8 == col8

    def gram(zz, k):
        cols = pl.ds(pl.multiple_of(1024 * zz + BLK * k, BLK), BLK)
        tok = raw[:, cols]
        return lax.dot_general(tok, tok, (((0,), (0,)), ((), ())), preferred_element_type=F32)

    def gram_step(i, first, last):
        zz = target(i)
        for k, (src, dst) in enumerate(parts(zz, c, low)):
            pltpu.make_async_copy(src, dst, s_loc.at[i, k]).wait()
        for k, (src, dst) in enumerate(parts(zz, c, high)):
            arrived(dst, s_raw_r.at[i, k])
        for xx in range(NX):
            one = gram(zz, 2 * xx)
            two = gram(zz, 2 * xx + 1)
            packed = jnp.where(upper, one, two).reshape(NY, 2, 8, BLK)
            extra = jnp.sum(jnp.where(middle, two, 0.0).reshape(16, 8, BLK), axis=0)
            ta[zz, xx, pl.ds(0, NY)] = packed[:, 0]
            ta[zz, xx, NY] = extra
            tile1 = packed[:, 1]
            if not first:
                arrived(rg.at[i - 2, xx], r_g.at[i - 2, xx])
                tile1 = tile1 + rg[i - 2, xx]
            if last:
                arrived(rg.at[i - 1, xx], r_g.at[i - 1, xx])
                tile1 = tile1 + rg[i - 1, xx]
            tg[zz, xx] = tile1
            if not last:
                send(tg.at[zz, xx], rg.at[i, xx], s_g.at[i, xx], r_g.at[i, xx], onward(i))
        for j in range(1, NX):
            to = (x + j) % NX
            send(ta.at[zz, to], ra.at[j - 1, zz], s_a.at[j - 1, i], r_a.at[j - 1, i], device(to, y, z, c))

    def tile0_step(i, first, last):
        zz = target(i)
        total = ta[zz, x]
        for j in range(NX - 1):
            arrived(ra.at[j, zz], r_a.at[j, i])
            total = total + ra[j, zz]
        if not first:
            arrived(rz.at[i - 2], r_z.at[i - 2])
            total = total + rz[i - 2]
        if last:
            arrived(rz.at[i - 1], r_z.at[i - 1])
            total = total + rz[i - 1]
        else:
            ta[zz, x] = total
            send(ta.at[zz, x], rz.at[i], s_z.at[i], r_z.at[i], onward(i))
        return total

    @pl.loop(0, 2)
    def _(i):
        gram_step(i, True, False)

    @pl.loop(2, 4)
    def _(i):
        gram_step(i, False, False)
        tile0_step(i - 2, True, False)

    @pl.loop(4, 7)
    def _(i):
        gram_step(i, False, False)
        tile0_step(i - 2, False, False)

    gram_step(7, False, True)
    for j in range(1, NX):
        to = (x + j) % NX
        send(tg.at[z, to], rx.at[j - 1], s_x.at[j - 1], r_x.at[j - 1], device(to, y, z, c))
    tile0_step(5, False, False)
    tile0_step(6, False, False)
    total0 = tile0_step(7, False, True)
    total1 = tg[z, x]
    for j in range(NX - 1):
        arrived(rx.at[j], r_x.at[j])
        total1 = total1 + rx[j]

    for yy in range(NY):
        a3[yy, 0] = total0[yy]
        a3[yy, 1] = total1[yy]
        a3[yy, 2] = total0[NY]
    for j in range(1, NY):
        to = (y + j) % NY
        send(a3.at[to], r3.at[j - 1], s_3.at[j - 1], r_3.at[j - 1], device(x, to, z, c))
    total = a3[y]
    for j in range(NY - 1):
        arrived(r3.at[j], r_3.at[j])
        total = total + r3[j]
    fin[...] = total[:2]
    d_out[...] = total[2]

    m_out[y] = total[:2]
    for j in range(1, NY):
        to = (y + j) % NY
        send(fin, m_out.at[y], s_f.at[j - 1], r_f.at[j - 1], device(x, to, z, c))
    for j in range(1, NY):
        arrived(m_out.at[(y - j + NY) % NY], r_f.at[j - 1])

    @pl.loop(0, NZ)
    def _(i):
        for k, (src, dst) in enumerate(parts(target(i), 1 - c, high)):
            arrived(src, s_raw_s.at[i, k])
        for j in range(NX - 1):
            arrived(ta.at[0, 0], s_a.at[j, i])

    @pl.loop(0, NZ - 1)
    def _(i):
        for xx in range(NX):
            arrived(tg.at[0, 0], s_g.at[i, xx])
        arrived(ta.at[0, 0], s_z.at[i])
        arrived(a3.at[0], s_3.at[i])
        arrived(fin, s_f.at[i])

    for j in range(NX - 1):
        arrived(tg.at[0, 0], s_x.at[j])


def gram_sums(hid, grd):
    dma = pltpu.SemaphoreType.DMA
    tile = (8, BLK)
    vm = pltpu.VMEM
    shapes = ((NZ, 2), (NX - 1, NZ), (NZ - 1,), (NZ - 1, NX), (NX - 1,), (NY - 1,), (NY - 1,))
    return pl.pallas_call(
        gram_kernel,
        out_shape=(jax.ShapeDtypeStruct((NY, 2) + tile, F32), jax.ShapeDtypeStruct(tile, F32)),
        in_specs=[pl.BlockSpec(memory_space=pl.ANY)] * 2,
        out_specs=[pl.BlockSpec(memory_space=pltpu.VMEM)] * 2,
        scratch_shapes=[
            vm((256, 8192), BF16),
            vm((NZ, NX, NY + 1) + tile, F32),
            vm((NZ, NX, NY) + tile, F32),
            vm((NX - 1, NZ, NY + 1) + tile, F32),
            vm((NZ - 1, NY + 1) + tile, F32),
            vm((NZ - 1, NX, NY) + tile, F32),
            vm((NX - 1, NY) + tile, F32),
            vm((NY, 3) + tile, F32),
            vm((NY - 1, 3) + tile, F32),
            vm((2,) + tile, F32),
            dma((NZ, 2)),
        ] + [dma(shape) for shape in shapes for _ in range(2)],
        compiler_params=pltpu.CompilerParams(
            collective_id=0, has_side_effects=True, vmem_limit_bytes=62 * 2**20
        ),
        cost_estimate=pl.CostEstimate(flops=2 * 64 * 256 * BLK * BLK, bytes_accessed=4 * 2**20, transcendentals=0),
        name="gram_sums",
    )(hid, grd)


def split3(value):
    high = value.astype(BF16)
    rest = value - high.astype(F32)
    mid = rest.astype(BF16)
    return high, mid, (rest - mid.astype(F32)).astype(BF16)


def product(left, right, fine):
    lh, lm, ll = split3(left)
    rh, rm, rl = split3(right)

    def dot(a, b):
        return jnp.dot(a, b, preferred_element_type=F32)

    if not fine:
        return dot(jnp.concatenate((lh, lm), axis=1), jnp.concatenate((rh, rh), axis=0)) + dot(lh, rm)
    small = dot(jnp.concatenate((lm, ll), axis=1), jnp.concatenate((rm, rh), axis=0))
    middle = dot(jnp.concatenate((lh, lm), axis=1), jnp.concatenate((rm, rh), axis=0))
    large = dot(jnp.concatenate((lh, lh), axis=1), jnp.concatenate((rh, rl), axis=0))
    return large + (middle + small)


def newton_kernel(token_total, m_hbm, d_hbm, x_hbm, m_ref, d_ref, x_ref, sem):
    loads = [pltpu.make_async_copy(m_hbm, m_ref, sem.at[0]), pltpu.make_async_copy(d_hbm, d_ref, sem.at[1])]
    for load in loads:
        load.start()
    for load in loads:
        load.wait()
    _, y, _, _ = place()
    second = (y % 2) == 1
    packed = m_ref[...].reshape(BLK, BLK)
    extra = jnp.broadcast_to(d_ref[...][None], (16, 8, BLK)).reshape(BLK, BLK)
    row = lax.broadcasted_iota(jnp.int32, (BLK, BLK), 0)
    col = lax.broadcasted_iota(jnp.int32, (BLK, BLK), 1)
    turned = packed.T
    first_block = jnp.where(row // 8 <= col // 8, packed, turned)
    second_block = jnp.where(row // 8 == col // 8, extra, jnp.where(row // 8 > col // 8, packed, turned))
    sums = jnp.where(second, second_block, first_block)
    identity = jnp.where(row == col, 1.0, 0.0)
    factor = sums / token_total + DAMPING * identity
    bound = jnp.max(jnp.sum(jnp.abs(factor), axis=1, keepdims=True), axis=0, keepdims=True)
    both = jnp.concatenate((factor / bound, identity / bound), axis=1)

    def refine(fine):
        return lambda step, both: 2.0 * both - product(both[:, :BLK], both, fine)

    both = lax.fori_loop(0, FINE, refine(True), both)
    both = lax.fori_loop(FINE, ITERS, refine(False), both)
    x_ref[...] = both[:, BLK:].astype(BF16)
    store = pltpu.make_async_copy(x_ref, x_hbm, sem.at[0])
    store.start()
    store.wait()


def newton(token_total, packed, extra):
    out = jax.ShapeDtypeStruct((BLK, BLK), BF16)
    return pl.pallas_call(
        lambda *refs: newton_kernel(token_total, *refs),
        out_shape=out,
        in_specs=[pl.BlockSpec(memory_space=pl.ANY)] * 2,
        out_specs=pl.BlockSpec(memory_space=pl.ANY),
        scratch_shapes=[pltpu.VMEM(a.shape, a.dtype) for a in (packed, extra, out)] + [pltpu.SemaphoreType.DMA((2,))],
        compiler_params=pltpu.CompilerParams(vmem_limit_bytes=62 * 2**20),
        name="newton",
    )(packed, extra)


def spread_kernel(inv, owner_a, owner_g, r4, rg, r5,
                  kept, sh, sg, s_l, s_p, r_p, s_z, r_z, s_k, r_k, s_q, r_q, s_4, r_4, s_g, r_g, s_5, r_5):
    x, y, z, c = place()
    own = lax.axis_index("own")
    yh, q = y // NYL, y % 2
    sib = device(x, y, z, 1 - c)
    beside = [device(x, (y + step) % NY, z, core) for core in (c, 1 - c) for step in (1, NY - 1)]

    barrier = pltpu.get_barrier_semaphore()
    for to in [sib] + beside:
        pl.semaphore_signal(barrier, inc=1, device_id=to, device_id_type=MESH)
    for j in range(1, NX):
        for core in (c, 1 - c):
            pl.semaphore_signal(barrier, inc=1, device_id=device((x + j) % NX, y, z, core), device_id_type=MESH)
    for j in range(1, NZ):
        pl.semaphore_signal(barrier, inc=1, device_id=device(x, y, (z + j) % NZ, c), device_id_type=MESH)

    mine_here = pltpu.make_async_copy(inv.at[pl.ds(pl.multiple_of(32 * x, 32), 32)], kept.at[c, q, z, x], s_l)
    mine_here.start()

    def find_a(b, found):
        at = owner_a[b] - 3 * own
        return tuple(jnp.where(at == k, b, found[k]) for k in range(3))

    def find_g(b, found):
        return jnp.where(owner_g[b] == own, b, found)

    zero = jnp.int32(0)
    slot_a = lax.fori_loop(0, 96, find_a, (zero, zero, zero))
    slot_g = lax.fori_loop(0, 32, find_g, zero)

    def at_a(b):
        return b // 48, b % 2, (b % 48) // 6, (b % 6) // 2

    def at_g(b):
        return b // 16, b % 2, (b % 16) // 2, 3

    want = [at_a(jnp.where(c == 0, slot_a[k], 3 * own + k)) for k in range(3)] + [at_g(slot_g)]
    mine_here.wait()
    pl.semaphore_wait(barrier, 5 + 2 * (NX - 1) + (NZ - 1))

    for j in range(1, NX):
        to = (x + j) % NX
        send(inv.at[pl.ds(pl.multiple_of(32 * to, 32), 32)], kept.at[c, q, z, x],
             s_p.at[j - 1], r_p.at[j - 1], device(to, y, z, c))
    for j in range(1, NX):
        arrived(kept.at[c, q, z, (x - j + NX) % NX], r_p.at[j - 1])
    for j in range(1, NZ):
        send(kept.at[c, q, z], kept.at[c, q, z], s_z.at[j - 1], r_z.at[j - 1], device(x, y, (z + j) % NZ, c))

    def pass_on(zz, j):
        for k in range(4):
            half = kept.at[c, q, zz, pl.ds(2 * (k % 2), 2)]
            send(half, half, s_q.at[j, k], r_q.at[j, k], beside[k])
        send(kept.at[c, q, zz], kept.at[c, q, zz], s_k.at[j], r_k.at[j], sib)

    pass_on(z, 0)
    for j in range(1, NZ):
        zz = (z - j + NZ) % NZ
        arrived(kept.at[c, q, zz], r_z.at[j - 1])
        pass_on(zz, j)
    for j in range(NZ):
        zz = (z - j + NZ) % NZ
        arrived(kept.at[1 - c, q, zz], r_k.at[j])
        for k in range(4):
            arrived(kept.at[(c + k // 2) % 2, 1 - q, zz, pl.ds(2 * (k % 2), 2)], r_q.at[j, k])

    for k in range(4):
        sh[k] = kept[want[k]]
    for j in range(1, NX + 1):
        to = (x + j) % NX
        for k in range(2):
            sg[to, k] = kept[at_g(8 * to + 4 * yh + 2 * c + k)]
        if j < NX:
            send(sh, r4.at[x], s_4.at[j - 1], r_4.at[j - 1], device(to, y, z, c))
            send(sh, r5.at[x], s_5.at[j - 1], r_5.at[j - 1], device(to, y, z, 1 - c))
            send(sg.at[to], rg.at[x], s_g.at[j - 1], r_g.at[j - 1], device(to, y, z, c))
    send(sh, r5.at[x], s_5.at[NX - 1], r_5.at[NX - 1], sib)
    r4[x] = sh[...]
    rg[x] = sg[x]
    for j in range(1, NX):
        frm = (x - j + NX) % NX
        arrived(r4.at[frm], r_4.at[j - 1])
        arrived(rg.at[frm], r_g.at[j - 1])
        arrived(r5.at[frm], r_5.at[j - 1])
    arrived(r5.at[x], r_5.at[NX - 1])

    for j in range(NZ):
        for k in range(4):
            arrived(kept.at[c, q, j, pl.ds(0, 2)], s_q.at[j, k])
        arrived(kept.at[c, q, j], s_k.at[j])
    for j in range(NZ - 1):
        arrived(kept.at[c, q, z], s_z.at[j])
    for j in range(NX - 1):
        arrived(kept.at[c, q, z, x], s_p.at[j])
        arrived(sh, s_4.at[j])
        arrived(sg.at[0], s_g.at[j])
    for j in range(NX):
        arrived(sh, s_5.at[j])


def spread(inv, owner_a, owner_g):
    dma = pltpu.SemaphoreType.DMA
    vm = pltpu.VMEM
    piece = (32, BLK)
    shapes = ((NX - 1,), (NZ - 1,), (NZ,), (NZ, 4), (NX - 1,), (NX - 1,), (NX,))
    return pl.pallas_call(
        spread_kernel,
        out_shape=tuple(jax.ShapeDtypeStruct((NX, n) + piece, BF16) for n in (4, 2, 4)),
        in_specs=[pl.BlockSpec(memory_space=pl.ANY)] + [pl.BlockSpec(memory_space=pltpu.SMEM)] * 2,
        out_specs=[pl.BlockSpec(memory_space=pltpu.VMEM)] * 3,
        scratch_shapes=[vm((2, 2, NZ, NX) + piece, BF16), vm((4,) + piece, BF16), vm((NX, 2) + piece, BF16), dma]
        + [dma(shape) for shape in shapes for _ in range(2)],
        compiler_params=pltpu.CompilerParams(
            collective_id=1, has_side_effects=True, vmem_limit_bytes=62 * 2**20
        ),
        name="spread_inverses",
    )(inv, owner_a, owner_g)


def apply_kernel(r4_hbm, rg_hbm, r5_hbm, w_hbm, a_hbm, g_hbm, p_hbm, r4, rg, r5, w, a_out, g_out, p_out, s_in, s_out):
    _, _, _, c = place()
    loads = [
        pltpu.make_async_copy(src, dst, s_in.at[k])
        for k, (src, dst) in enumerate(((r4_hbm, r4), (rg_hbm, rg), (r5_hbm, r5), (w_hbm, w)))
    ]
    for load in loads:
        load.start()
    for load in loads:
        load.wait()

    def whole(ref, k):
        return ref[:, k].reshape(BLK, BLK)

    mine = [whole(r4, k) for k in range(4)]
    right = [whole(rg, k) for k in range(2)]
    theirs = [whole(r5, k) for k in range(4)]
    core0 = c == 0
    stores = []

    def store(src, dst):
        stores.append(pltpu.make_async_copy(src, dst, s_out.at[len(stores)]))
        stores[-1].start()

    for k in range(3):
        placed = jnp.where(core0, theirs[k], mine[k])
        rows = pl.ds(BLK * k, BLK)
        left = jnp.dot(placed, w[rows, :], preferred_element_type=F32).astype(BF16)
        for m in range(2):
            cols = slice(BLK * m, BLK * (m + 1))
            p_out[rows, cols] = jnp.dot(left[:, cols], right[m], preferred_element_type=F32)
        store(p_out.at[rows], p_hbm.at[rows])
    for k in range(3):
        a_out[k] = jnp.where(core0, mine[k], theirs[k])
    store(a_out, a_hbm)
    g_out[0] = mine[3]
    store(g_out, g_hbm)
    for each in stores:
        each.wait()


def apply_inverses(r4, rg, r5, w):
    outs = (
        jax.ShapeDtypeStruct((3, BLK, BLK), BF16),
        jax.ShapeDtypeStruct((1, BLK, BLK), BF16),
        jax.ShapeDtypeStruct(w.shape, F32),
    )
    return pl.pallas_call(
        apply_kernel,
        out_shape=outs,
        in_specs=[pl.BlockSpec(memory_space=pl.ANY)] * 4,
        out_specs=[pl.BlockSpec(memory_space=pl.ANY)] * 3,
        scratch_shapes=[pltpu.VMEM(a.shape, a.dtype) for a in (r4, rg, r5, w) + outs]
        + [pltpu.SemaphoreType.DMA((4,)), pltpu.SemaphoreType.DMA((5,))],
        compiler_params=pltpu.CompilerParams(vmem_limit_bytes=62 * 2**20),
        name="apply_inverses",
    )(r4, rg, r5, w)


def on_device(hidden_act, out_grad, weight_grad, owner_a, owner_g):
    token_total = hidden_act.shape[0] * lax.axis_size("own") * lax.axis_size("dp")
    packed, extra = gram_sums(hidden_act, out_grad)
    inverse = newton(token_total, packed, extra)
    return apply_inverses(*spread(inverse, owner_a, owner_g), weight_grad)


def solution(mesh):
    placed = (P(("dp", "own"), None), P(("dp", "own"), None), P("own", "dp"), P(), P())
    return jax.shard_map(
        on_device,
        mesh=mesh,
        in_specs=placed,
        out_specs=(P("own", None, None), P("own", None, None), P("own", "dp")),
        check_vma=False,
    )
```

```python
import jax
import jax.numpy as jnp
from jax import lax
from jax.experimental import pallas as pl
from jax.experimental.pallas import tpu as pltpu
from jax.sharding import PartitionSpec as P

BLK = 128
ITERS = 14
FINE = 4
DAMPING = 0.05
NX, NY, NZ, NYL = 4, 8, 8, 4
MESH = pl.DeviceIdType.MESH
F32 = jnp.float32
BF16 = jnp.bfloat16


FAR_FIRST = (4, 3, 5, 2, 6, 1, 7)


def mod(value, n):
    return value % n if isinstance(value, int) else lax.rem(value, n)


class Place:
    def __init__(self):
        self.dp, self.own = lax.axis_index("dp"), lax.axis_index("own")
        self.x, self.c = lax.div(self.dp, 4), mod(self.dp, 2)
        self.yh = mod(lax.div(self.dp, 2), 2)
        self.z, self.yl = lax.div(self.own, NYL), mod(self.own, NYL)
        self.y = self.yh * NYL + self.yl

    def at_x(self, to):
        return (self.dp + 4 * (to - self.x), self.own)

    def at_y(self, to):
        return (self.dp + 2 * (lax.div(to, NYL) - self.yh), self.own + mod(to, NYL) - self.yl)

    def at_z(self, to):
        return (self.dp, self.own + NYL * (to - self.z))

    def other_core(self):
        return (self.dp + 1 - 2 * self.c, self.own)


def send(src, dst, send_sem, recv_sem, to):
    copy = pltpu.make_async_remote_copy(
        src_ref=src, dst_ref=dst, send_sem=send_sem, recv_sem=recv_sem,
        device_id=to, device_id_type=MESH,
    )
    copy.start()


def arrived(ref, sem):
    pltpu.make_async_copy(ref, ref, sem).wait()


def gram_kernel(hid, grd, m_out, d_out,
                raw, ta, tg, ra, rz, rg, rx, a3, r3, fin,
                s_loc, s_raw_s, s_raw_r, s_a, r_a, s_z, r_z, s_g, r_g, s_x, r_x, s_3, r_3, s_f, r_f):
    here = Place()
    x, y, z, c = here.x, here.y, here.z, here.c
    sib = here.other_core()

    barrier = pltpu.get_barrier_semaphore()
    pl.semaphore_signal(barrier, inc=1, device_id=sib, device_id_type=MESH)
    for j in range(1, NX):
        pl.semaphore_signal(barrier, inc=1, device_id=here.at_x(mod(x + j, NX)), device_id_type=MESH)
    for j in range(1, NY):
        pl.semaphore_signal(barrier, inc=1, device_id=here.at_y(mod(y + j, NY)), device_id_type=MESH)
    for j in (1, NZ - 1):
        pl.semaphore_signal(barrier, inc=1, device_id=here.at_z(mod(z + j, NZ)), device_id_type=MESH)

    def target(i):
        return mod(z + 4 + (2 * mod(i, 2) - 1) * ((i + 1) // 2 if isinstance(i, int) else lax.div(i + 1, 2)), NZ)

    def onward(i):
        return here.at_z(mod(z + NZ + 1 - 2 * mod(i, 2), NZ))

    def parts(zz, core, rows):
        return (
            (hid.at[:, pl.ds(pl.multiple_of(6144 * core + 768 * zz, 128), 768)],
             raw.at[rows, pl.ds(pl.multiple_of(1024 * zz, 128), 768)]),
            (grd.at[:, pl.ds(pl.multiple_of(2048 * core + 256 * zz, 128), 256)],
             raw.at[rows, pl.ds(pl.multiple_of(1024 * zz + 768, 128), 256)]),
        )

    low, high = pl.ds(0, 128), pl.ds(128, 128)

    @pl.loop(0, NZ)
    def _(i):
        for k, (src, dst) in enumerate(parts(target(i), c, low)):
            pltpu.make_async_copy(src, dst, s_loc.at[i, k]).start()

    pl.semaphore_wait(barrier, 1 + (NX - 1) + (NY - 1) + 2)

    @pl.loop(0, NZ)
    def _(i):
        for k, (src, dst) in enumerate(parts(target(i), 1 - c, high)):
            send(src, dst, s_raw_s.at[i, k], s_raw_r.at[i, k], sib)

    row8 = lax.broadcasted_iota(jnp.int32, (BLK, BLK), 0) // 8
    col8 = lax.broadcasted_iota(jnp.int32, (BLK, BLK), 1) // 8
    upper = row8 <= col8
    middle = row8 == col8

    def gram(zz, k):
        cols = pl.ds(pl.multiple_of(1024 * zz + BLK * k, BLK), BLK)
        tok = raw[:, cols]
        return lax.dot_general(tok, tok, (((0,), (0,)), ((), ())), preferred_element_type=F32)

    def gram_step(i, first, last):
        zz = target(i)
        for k, (src, dst) in enumerate(parts(zz, c, low)):
            pltpu.make_async_copy(src, dst, s_loc.at[i, k]).wait()
        for k, (src, dst) in enumerate(parts(zz, c, high)):
            arrived(dst, s_raw_r.at[i, k])
        for xx in range(NX):
            one = gram(zz, 2 * xx)
            two = gram(zz, 2 * xx + 1)
            packed = jnp.where(upper, one, two).reshape(NY, 2, 8, BLK)
            extra = jnp.sum(jnp.where(middle, two, 0.0).reshape(16, 8, BLK), axis=0)
            ta[zz, xx, pl.ds(0, NY)] = packed[:, 0]
            ta[zz, xx, NY] = extra
            tg[zz, xx] = packed[:, 1]
        for j in (2, 1, 3):
            to = mod(x + j, NX)
            send(ta.at[zz, to], ra.at[j - 1, zz], s_a.at[j - 1, i], r_a.at[j - 1, i], here.at_x(to))
        for xx in range(NX):
            if not first:
                arrived(rg.at[i - 2, xx], r_g.at[i - 2, xx])
                tile1 = tg[zz, xx] + rg[i - 2, xx]
                if last:
                    arrived(rg.at[i - 1, xx], r_g.at[i - 1, xx])
                    tile1 = tile1 + rg[i - 1, xx]
                tg[zz, xx] = tile1
            if not last:
                send(tg.at[zz, xx], rg.at[i, xx], s_g.at[i, xx], r_g.at[i, xx], onward(i))

    def tile0_step(i, first, last):
        zz = target(i)
        total = ta[zz, x]
        for j in range(NX - 1):
            arrived(ra.at[j, zz], r_a.at[j, i])
            total = total + ra[j, zz]
        if not first:
            arrived(rz.at[i - 2], r_z.at[i - 2])
            total = total + rz[i - 2]
        if last:
            arrived(rz.at[i - 1], r_z.at[i - 1])
            total = total + rz[i - 1]
        else:
            ta[zz, x] = total
            send(ta.at[zz, x], rz.at[i], s_z.at[i], r_z.at[i], onward(i))
        return total

    @pl.loop(0, 2)
    def _(i):
        gram_step(i, True, False)

    @pl.loop(2, 4)
    def _(i):
        gram_step(i, False, False)
        tile0_step(i - 2, True, False)

    @pl.loop(4, 7)
    def _(i):
        gram_step(i, False, False)
        tile0_step(i - 2, False, False)

    gram_step(7, False, True)
    for j in (2, 1, 3):
        to = mod(x + j, NX)
        send(tg.at[z, to], rx.at[j - 1], s_x.at[j - 1], r_x.at[j - 1], here.at_x(to))
    tile0_step(5, False, False)
    tile0_step(6, False, False)
    total0 = tile0_step(7, False, True)
    total1 = tg[z, x]
    for j in range(NX - 1):
        arrived(rx.at[j], r_x.at[j])
        total1 = total1 + rx[j]

    for yy in range(NY):
        a3[yy, 0] = total0[yy]
        a3[yy, 1] = total1[yy]
        a3[yy, 2] = total0[NY]
    for j in FAR_FIRST:
        to = mod(y + j, NY)
        send(a3.at[to], r3.at[j - 1], s_3.at[j - 1], r_3.at[j - 1], here.at_y(to))
    total = a3[y]
    for j in range(NY - 1):
        arrived(r3.at[j], r_3.at[j])
        total = total + r3[j]
    fin[...] = total[:2]
    d_out[...] = total[2]

    m_out[y] = total[:2]
    for j in FAR_FIRST:
        send(fin, m_out.at[y], s_f.at[j - 1], r_f.at[j - 1], here.at_y(mod(y + j, NY)))
    for j in range(1, NY):
        arrived(m_out.at[mod(y - j + NY, NY)], r_f.at[j - 1])

    @pl.loop(0, NZ)
    def _(i):
        for k, (src, dst) in enumerate(parts(target(i), 1 - c, high)):
            arrived(src, s_raw_s.at[i, k])
        for j in range(NX - 1):
            arrived(ta.at[0, 0], s_a.at[j, i])

    @pl.loop(0, NZ - 1)
    def _(i):
        for xx in range(NX):
            arrived(tg.at[0, 0], s_g.at[i, xx])
        arrived(ta.at[0, 0], s_z.at[i])
        arrived(a3.at[0], s_3.at[i])
        arrived(fin, s_f.at[i])

    for j in range(NX - 1):
        arrived(tg.at[0, 0], s_x.at[j])


def gram_sums(hid, grd):
    dma = pltpu.SemaphoreType.DMA
    tile = (8, BLK)
    vm = pltpu.VMEM
    shapes = ((NZ, 2), (NX - 1, NZ), (NZ - 1,), (NZ - 1, NX), (NX - 1,), (NY - 1,), (NY - 1,))
    return pl.pallas_call(
        gram_kernel,
        out_shape=(jax.ShapeDtypeStruct((NY, 2) + tile, F32), jax.ShapeDtypeStruct(tile, F32)),
        in_specs=[pl.BlockSpec(memory_space=pl.ANY)] * 2,
        out_specs=[pl.BlockSpec(memory_space=pltpu.VMEM)] * 2,
        scratch_shapes=[
            vm((256, 8192), BF16),
            vm((NZ, NX, NY + 1) + tile, F32),
            vm((NZ, NX, NY) + tile, F32),
            vm((NX - 1, NZ, NY + 1) + tile, F32),
            vm((NZ - 1, NY + 1) + tile, F32),
            vm((NZ - 1, NX, NY) + tile, F32),
            vm((NX - 1, NY) + tile, F32),
            vm((NY, 3) + tile, F32),
            vm((NY - 1, 3) + tile, F32),
            vm((2,) + tile, F32),
            dma((NZ, 2)),
        ] + [dma(shape) for shape in shapes for _ in range(2)],
        compiler_params=pltpu.CompilerParams(
            collective_id=0, has_side_effects=True, vmem_limit_bytes=62 * 2**20
        ),
        cost_estimate=pl.CostEstimate(flops=2 * 64 * 256 * BLK * BLK, bytes_accessed=4 * 2**20, transcendentals=0),
        name="gram_sums",
    )(hid, grd)


def split3(value):
    high = value.astype(BF16)
    rest = value - high.astype(F32)
    mid = rest.astype(BF16)
    return high, mid, (rest - mid.astype(F32)).astype(BF16)


def product(left, right, fine):
    lh, lm, ll = split3(left)
    rh, rm, rl = split3(right)

    def dot(a, b):
        return jnp.dot(a, b, preferred_element_type=F32)

    if not fine:
        return dot(jnp.concatenate((lh, lm), axis=1), jnp.concatenate((rh, rh), axis=0)) + dot(lh, rm)
    small = dot(jnp.concatenate((lm, ll), axis=1), jnp.concatenate((rm, rh), axis=0))
    middle = dot(jnp.concatenate((lh, lm), axis=1), jnp.concatenate((rm, rh), axis=0))
    large = dot(jnp.concatenate((lh, lh), axis=1), jnp.concatenate((rh, rl), axis=0))
    return large + (middle + small)


def newton_kernel(token_total, m_hbm, d_hbm, x_hbm, m_ref, d_ref, x_ref, sem):
    loads = [pltpu.make_async_copy(m_hbm, m_ref, sem.at[0]), pltpu.make_async_copy(d_hbm, d_ref, sem.at[1])]
    for load in loads:
        load.start()
    for load in loads:
        load.wait()
    second = mod(Place().y, 2) == 1
    packed = m_ref[...].reshape(BLK, BLK)
    extra = jnp.broadcast_to(d_ref[...][None], (16, 8, BLK)).reshape(BLK, BLK)
    row = lax.broadcasted_iota(jnp.int32, (BLK, BLK), 0)
    col = lax.broadcasted_iota(jnp.int32, (BLK, BLK), 1)
    turned = packed.T
    first_block = jnp.where(row // 8 <= col // 8, packed, turned)
    second_block = jnp.where(row // 8 == col // 8, extra, jnp.where(row // 8 > col // 8, packed, turned))
    sums = jnp.where(second, second_block, first_block)
    identity = jnp.where(row == col, 1.0, 0.0)
    factor = sums / token_total + DAMPING * identity
    bound = jnp.max(jnp.sum(jnp.abs(factor), axis=1, keepdims=True), axis=0, keepdims=True)
    both = jnp.concatenate((factor / bound, identity / bound), axis=1)

    def refine(fine):
        return lambda step, both: 2.0 * both - product(both[:, :BLK], both, fine)

    both = lax.fori_loop(0, FINE, refine(True), both)
    both = lax.fori_loop(FINE, ITERS, refine(False), both)
    x_ref[...] = both[:, BLK:].astype(BF16)
    store = pltpu.make_async_copy(x_ref, x_hbm, sem.at[0])
    store.start()
    store.wait()


def newton(token_total, packed, extra):
    out = jax.ShapeDtypeStruct((BLK, BLK), BF16)
    return pl.pallas_call(
        lambda *refs: newton_kernel(token_total, *refs),
        out_shape=out,
        in_specs=[pl.BlockSpec(memory_space=pl.ANY)] * 2,
        out_specs=pl.BlockSpec(memory_space=pl.ANY),
        scratch_shapes=[pltpu.VMEM(a.shape, a.dtype) for a in (packed, extra, out)] + [pltpu.SemaphoreType.DMA((2,))],
        compiler_params=pltpu.CompilerParams(vmem_limit_bytes=62 * 2**20),
        name="newton",
    )(packed, extra)


def spread_kernel(inv, owner_a, owner_g, r4, r5,
                  kept, es, er, s4, s_l, s_p, r_p, s_z, r_z, s_q, r_q, s_e, r_e, s_4, r_4, s_5, r_5):
    here = Place()
    x, y, z, c, yh, own = here.x, here.y, here.z, here.c, here.yh, here.own
    q = mod(y, 2)
    sib = here.other_core()
    beside = [here.at_y(mod(y + step, NY)) for step in (1, NY - 1)]

    barrier = pltpu.get_barrier_semaphore()
    for to in [sib] + beside:
        pl.semaphore_signal(barrier, inc=1, device_id=to, device_id_type=MESH)
    for j in range(1, NX):
        pl.semaphore_signal(barrier, inc=1, device_id=here.at_x(mod(x + j, NX)), device_id_type=MESH)
    for j in range(1, NZ):
        pl.semaphore_signal(barrier, inc=1, device_id=here.at_z(mod(z + j, NZ)), device_id_type=MESH)

    mine_here = pltpu.make_async_copy(inv.at[pl.ds(pl.multiple_of(32 * x, 32), 32)], kept.at[q, z, x], s_l)
    mine_here.start()
    pl.semaphore_wait(barrier, 1 + (NX - 1) + 2 + (NZ - 1))
    for j in (2, 1, 3):
        to = mod(x + j, NX)
        send(inv.at[pl.ds(pl.multiple_of(32 * to, 32), 32)], kept.at[q, z, x],
             s_p.at[j - 1], r_p.at[j - 1], here.at_x(to))
    mine_here.wait()
    for j in range(1, NX):
        arrived(kept.at[q, z, mod(x - j + NX, NX)], r_p.at[j - 1])
    for j in FAR_FIRST:
        send(kept.at[q, z], kept.at[q, z], s_z.at[j - 1], r_z.at[j - 1], here.at_z(mod(z + j, NZ)))

    def to_neighbours(zz, j):
        for k in range(2):
            half = kept.at[q, zz, pl.ds(2 * k, 2)]
            send(half, half, s_q.at[j, k], r_q.at[j, k], beside[k])

    to_neighbours(z, 0)

    def find_a(b, found):
        at = owner_a[b] - 3 * own
        return tuple(jnp.where(at == k, b, found[k]) for k in range(3))

    def find_g(b, found):
        return jnp.where(owner_g[b] == own, b, found)

    zero = jnp.int32(0)
    slot_a = lax.fori_loop(0, 96, find_a, (zero, zero, zero))
    slot_g = lax.fori_loop(0, 32, find_g, zero)

    def at_a(b):
        return mod(b, 2), lax.div(mod(b, 48), 6), lax.div(mod(b, 6), 2)

    def at_g(b):
        return mod(b, 2), lax.div(mod(b, 16), 2), 3

    def entry(core, k):
        if k == 3:
            return lax.div(slot_g, 16), at_g(slot_g)
        block = jnp.where(core == 0, slot_a[k], 3 * own + k)
        return lax.div(block, 48), at_a(block)

    mine = [entry(c, k) for k in range(4)]
    theirs = [entry(1 - c, k) for k in range(4)]
    for j in FAR_FIRST:
        zz = mod(z - j + NZ, NZ)
        arrived(kept.at[q, zz], r_z.at[j - 1])
        to_neighbours(zz, j)
    for j in range(NZ):
        zz = mod(z - j + NZ, NZ)
        for k in range(2):
            arrived(kept.at[1 - q, zz, pl.ds(2 * k, 2)], r_q.at[j, k])

    for k in range(4):
        es[k] = kept[theirs[k][1]]
    for m in range(2):
        for k in range(2):
            es[4 + 2 * m + k] = kept[at_g(8 * (2 * c + m) + 4 * yh + 2 * (1 - c) + k)]
    send(es, er, s_e.at[0], r_e.at[0], sib)
    values = [kept[mine[k][1]] for k in range(4)]
    arrived(er, r_e.at[0])
    values = [jnp.where(mine[k][0] == c, values[k], er[k]) for k in range(4)]
    for j in range(1, NX + 1):
        to = mod(x + j, NX)
        for k in range(4):
            s4[to, k] = values[k]
        for k in range(2):
            own_half = kept[at_g(8 * to + 4 * yh + 2 * c + k)]
            s4[to, 4 + k] = jnp.where(lax.div(to, 2) == c, own_half, er[4 + 2 * mod(to, 2) + k])
        if j < NX:
            send(s4.at[to], r4.at[x], s_4.at[j - 1], r_4.at[j - 1], here.at_x(to))
    r4[x] = s4[x]
    send(s4.at[x, pl.ds(0, 4)], r5.at[x], s_5.at[0], r_5.at[0], sib)
    for j in range(1, NX):
        frm = mod(x - j + NX, NX)
        arrived(r4.at[frm], r_4.at[j - 1])
        send(r4.at[frm, pl.ds(0, 4)], r5.at[frm], s_5.at[j], r_5.at[j], sib)
    for j in range(NX):
        arrived(r5.at[mod(x - j + NX, NX)], r_5.at[j])

    for j in range(NZ):
        for k in range(2):
            arrived(kept.at[q, j, pl.ds(2 * k, 2)], s_q.at[j, k])
    for j in range(NZ - 1):
        arrived(kept.at[q, z], s_z.at[j])
    for j in range(NX - 1):
        arrived(kept.at[q, z, x], s_p.at[j])
        arrived(s4.at[j], s_4.at[j])
    arrived(es, s_e.at[0])
    for j in range(NX):
        arrived(r5.at[j], s_5.at[j])


def spread(inv, owner_a, owner_g):
    dma = pltpu.SemaphoreType.DMA
    vm = pltpu.VMEM
    piece = (32, BLK)
    shapes = ((NX - 1,), (NZ - 1,), (NZ, 2), (1,), (NX - 1,), (NX,))
    return pl.pallas_call(
        spread_kernel,
        out_shape=(jax.ShapeDtypeStruct((NX, 6) + piece, BF16), jax.ShapeDtypeStruct((NX, 4) + piece, BF16)),
        in_specs=[pl.BlockSpec(memory_space=pl.ANY)] + [pl.BlockSpec(memory_space=pltpu.SMEM)] * 2,
        out_specs=[pl.BlockSpec(memory_space=pltpu.VMEM)] * 2,
        scratch_shapes=[
            vm((2, NZ, NX) + piece, BF16), vm((8,) + piece, BF16), vm((8,) + piece, BF16), vm((NX, 6) + piece, BF16), dma,
        ] + [dma(shape) for shape in shapes for _ in range(2)],
        compiler_params=pltpu.CompilerParams(
            collective_id=1, has_side_effects=True, vmem_limit_bytes=62 * 2**20
        ),
        name="spread_inverses",
    )(inv, owner_a, owner_g)


def apply_kernel(r4_hbm, r5_hbm, w_hbm, a_hbm, g_hbm, p_hbm, r4, r5, w, a_out, g_out, p_out, s_in, s_out):
    c = Place().c
    loads = [
        pltpu.make_async_copy(src, dst, s_in.at[k])
        for k, (src, dst) in enumerate(((r4_hbm, r4), (r5_hbm, r5), (w_hbm, w)))
    ]
    for load in loads:
        load.start()
    for load in loads:
        load.wait()

    def whole(ref, k):
        return ref[:, k].reshape(BLK, BLK)

    mine = [whole(r4, k) for k in range(6)]
    theirs = [whole(r5, k) for k in range(4)]
    core0 = c == 0
    stores = []

    def store(src, dst):
        stores.append(pltpu.make_async_copy(src, dst, s_out.at[len(stores)]))
        stores[-1].start()

    for k in range(3):
        placed = jnp.where(core0, theirs[k], mine[k])
        rows = pl.ds(BLK * k, BLK)
        left = jnp.dot(placed, w[rows, :], preferred_element_type=F32).astype(BF16)
        for m in range(2):
            cols = slice(BLK * m, BLK * (m + 1))
            p_out[rows, cols] = jnp.dot(left[:, cols], mine[4 + m], preferred_element_type=F32)
        store(p_out.at[rows], p_hbm.at[rows])
    for k in range(3):
        a_out[k] = jnp.where(core0, mine[k], theirs[k])
    store(a_out, a_hbm)
    g_out[0] = mine[3]
    store(g_out, g_hbm)
    for each in stores:
        each.wait()


def apply_inverses(r4, r5, w):
    outs = (
        jax.ShapeDtypeStruct((3, BLK, BLK), BF16),
        jax.ShapeDtypeStruct((1, BLK, BLK), BF16),
        jax.ShapeDtypeStruct(w.shape, F32),
    )
    return pl.pallas_call(
        apply_kernel,
        out_shape=outs,
        in_specs=[pl.BlockSpec(memory_space=pl.ANY)] * 3,
        out_specs=[pl.BlockSpec(memory_space=pl.ANY)] * 3,
        scratch_shapes=[pltpu.VMEM(a.shape, a.dtype) for a in (r4, r5, w) + outs]
        + [pltpu.SemaphoreType.DMA((3,)), pltpu.SemaphoreType.DMA((5,))],
        compiler_params=pltpu.CompilerParams(vmem_limit_bytes=62 * 2**20),
        name="apply_inverses",
    )(r4, r5, w)


def on_device(hidden_act, out_grad, weight_grad, owner_a, owner_g):
    token_total = hidden_act.shape[0] * lax.axis_size("own") * lax.axis_size("dp")
    packed, extra = gram_sums(hidden_act, out_grad)
    inverse = newton(token_total, packed, extra)
    return apply_inverses(*spread(inverse, owner_a, owner_g), weight_grad)


def solution(mesh):
    placed = (P(("dp", "own"), None), P(("dp", "own"), None), P("own", "dp"), P(), P())
    return jax.shard_map(
        on_device,
        mesh=mesh,
        in_specs=placed,
        out_specs=(P("own", None, None), P("own", None, None), P("own", "dp")),
        check_vma=False,
    )
```

```python
import jax
import jax.numpy as jnp
from jax import lax
from jax.experimental import pallas as pl
from jax.experimental.pallas import tpu as pltpu
from jax.sharding import PartitionSpec as P

BLK = 128
ITERS = 14
FINE = 4
DAMPING = 0.05
NX, NY, NZ, NYL = 4, 8, 8, 4
MESH = pl.DeviceIdType.MESH
F32 = jnp.float32
BF16 = jnp.bfloat16


FAR_FIRST = (4, 3, 5, 2, 6, 1, 7)


def mod(value, n):
    return value % n if isinstance(value, int) else lax.rem(value, n)


class Place:
    def __init__(self):
        self.dp, self.own = lax.axis_index("dp"), lax.axis_index("own")
        self.x, self.c = lax.div(self.dp, 4), mod(self.dp, 2)
        self.yh = mod(lax.div(self.dp, 2), 2)
        self.z, self.yl = lax.div(self.own, NYL), mod(self.own, NYL)
        self.y = self.yh * NYL + self.yl

    def at_x(self, to):
        return (self.dp + 4 * (to - self.x), self.own)

    def at_y(self, to):
        return (self.dp + 2 * (lax.div(to, NYL) - self.yh), self.own + mod(to, NYL) - self.yl)

    def at_z(self, to):
        return (self.dp, self.own + NYL * (to - self.z))

    def other_core(self):
        return (self.dp + 1 - 2 * self.c, self.own)


def send(src, dst, send_sem, recv_sem, to):
    copy = pltpu.make_async_remote_copy(
        src_ref=src, dst_ref=dst, send_sem=send_sem, recv_sem=recv_sem,
        device_id=to, device_id_type=MESH,
    )
    copy.start()


def arrived(ref, sem):
    pltpu.make_async_copy(ref, ref, sem).wait()


def gram_kernel(hid, grd, m_out, d_out,
                raw, ta, tg, ru, rv, rw, rz, rg, rx, a3, r3, fin,
                s_loc, s_raw_s, s_raw_r, s_a, r_a, s_z, r_z, s_g, r_g, s_x, r_x, s_3, r_3, s_f, r_f):
    here = Place()
    x, y, z, c = here.x, here.y, here.z, here.c
    sib = here.other_core()

    barrier = pltpu.get_barrier_semaphore()
    pl.semaphore_signal(barrier, inc=1, device_id=sib, device_id_type=MESH)
    for j in range(1, NX):
        pl.semaphore_signal(barrier, inc=1, device_id=here.at_x(mod(x + j, NX)), device_id_type=MESH)
    for j in range(1, NY):
        pl.semaphore_signal(barrier, inc=1, device_id=here.at_y(mod(y + j, NY)), device_id_type=MESH)
    for j in (1, NZ - 1):
        pl.semaphore_signal(barrier, inc=1, device_id=here.at_z(mod(z + j, NZ)), device_id_type=MESH)

    def target(i):
        return mod(z + 4 + (2 * mod(i, 2) - 1) * ((i + 1) // 2 if isinstance(i, int) else lax.div(i + 1, 2)), NZ)

    def onward(i):
        return here.at_z(mod(z + NZ + 1 - 2 * mod(i, 2), NZ))

    def x_ways(i):
        turn = 2 * mod(i, 2)
        return mod(x + 1 + turn, NX), mod(x + 3 - turn, NX)

    def parts(zz, core, rows):
        return (
            (hid.at[:, pl.ds(pl.multiple_of(6144 * core + 768 * zz, 128), 768)],
             raw.at[rows, pl.ds(pl.multiple_of(1024 * zz, 128), 768)]),
            (grd.at[:, pl.ds(pl.multiple_of(2048 * core + 256 * zz, 128), 256)],
             raw.at[rows, pl.ds(pl.multiple_of(1024 * zz + 768, 128), 256)]),
        )

    low, high = pl.ds(0, 128), pl.ds(128, 128)

    @pl.loop(0, NZ)
    def _(i):
        for k, (src, dst) in enumerate(parts(target(i), c, low)):
            pltpu.make_async_copy(src, dst, s_loc.at[i, k]).start()

    pl.semaphore_wait(barrier, 1 + (NX - 1) + (NY - 1) + 2)

    @pl.loop(0, NZ)
    def _(i):
        for k, (src, dst) in enumerate(parts(target(i), 1 - c, high)):
            send(src, dst, s_raw_s.at[i, k], s_raw_r.at[i, k], sib)

    row8 = lax.broadcasted_iota(jnp.int32, (BLK, BLK), 0) // 8
    col8 = lax.broadcasted_iota(jnp.int32, (BLK, BLK), 1) // 8
    upper = row8 <= col8
    middle = row8 == col8

    def gram(zz, k):
        cols = pl.ds(pl.multiple_of(1024 * zz + BLK * k, BLK), BLK)
        tok = raw[:, cols]
        return lax.dot_general(tok, tok, (((0,), (0,)), ((), ())), preferred_element_type=F32)

    def gram_step(i, first, last):
        zz = target(i)
        for k, (src, dst) in enumerate(parts(zz, c, low)):
            pltpu.make_async_copy(src, dst, s_loc.at[i, k]).wait()
        for k, (src, dst) in enumerate(parts(zz, c, high)):
            arrived(dst, s_raw_r.at[i, k])
        for xx in range(NX):
            one = gram(zz, 2 * xx)
            two = gram(zz, 2 * xx + 1)
            packed = jnp.where(upper, one, two).reshape(NY, 2, 8, BLK)
            extra = jnp.sum(jnp.where(middle, two, 0.0).reshape(16, 8, BLK), axis=0)
            ta[zz, xx, pl.ds(0, NY)] = packed[:, 0]
            ta[zz, xx, NY] = extra
            tg[zz, xx] = packed[:, 1]
        ahead, back = x_ways(i)
        send(ta.at[zz, mod(x + 2, NX)], ru.at[i], s_a.at[0, i], r_a.at[0, i], here.at_x(ahead))
        send(ta.at[zz, back], rv.at[i], s_a.at[1, i], r_a.at[1, i], here.at_x(back))
        for xx in range(NX):
            if not first:
                arrived(rg.at[i - 2, xx], r_g.at[i - 2, xx])
                tile1 = tg[zz, xx] + rg[i - 2, xx]
                if last:
                    arrived(rg.at[i - 1, xx], r_g.at[i - 1, xx])
                    tile1 = tile1 + rg[i - 1, xx]
                tg[zz, xx] = tile1
            if not last:
                send(tg.at[zz, xx], rg.at[i, xx], s_g.at[i, xx], r_g.at[i, xx], onward(i))

    def x_step(i):
        zz = target(i)
        ahead, _ = x_ways(i)
        arrived(ru.at[i], r_a.at[0, i])
        ta[zz, ahead] = ta[zz, ahead] + ru[i]
        send(ta.at[zz, ahead], rw.at[i], s_a.at[2, i], r_a.at[2, i], here.at_x(ahead))

    def tile0_step(i, first, last):
        zz = target(i)
        arrived(rv.at[i], r_a.at[1, i])
        arrived(rw.at[i], r_a.at[2, i])
        total = ta[zz, x] + rv[i] + rw[i]
        if not first:
            arrived(rz.at[i - 2], r_z.at[i - 2])
            total = total + rz[i - 2]
        if last:
            arrived(rz.at[i - 1], r_z.at[i - 1])
            total = total + rz[i - 1]
        else:
            ta[zz, x] = total
            send(ta.at[zz, x], rz.at[i], s_z.at[i], r_z.at[i], onward(i))
        return total

    @pl.loop(0, 2)
    def _(i):
        gram_step(i, True, False)

    gram_step(2, False, False)
    x_step(0)
    x_step(1)

    @pl.loop(3, 5)
    def _(i):
        gram_step(i, False, False)
        x_step(i - 1)
        tile0_step(i - 3, True, False)

    @pl.loop(5, 7)
    def _(i):
        gram_step(i, False, False)
        x_step(i - 1)
        tile0_step(i - 3, False, False)

    gram_step(7, False, True)
    for j in (2, 1, 3):
        to = mod(x + j, NX)
        send(tg.at[z, to], rx.at[j - 1], s_x.at[j - 1], r_x.at[j - 1], here.at_x(to))
    x_step(6)
    tile0_step(4, False, False)
    tile0_step(5, False, False)
    x_step(7)
    tile0_step(6, False, False)
    total0 = tile0_step(7, False, True)
    total1 = tg[z, x]
    for j in range(NX - 1):
        arrived(rx.at[j], r_x.at[j])
        total1 = total1 + rx[j]

    for yy in range(NY):
        a3[yy, 0] = total0[yy]
        a3[yy, 1] = total1[yy]
        a3[yy, 2] = total0[NY]
    for j in FAR_FIRST:
        to = mod(y + j, NY)
        send(a3.at[to], r3.at[j - 1], s_3.at[j - 1], r_3.at[j - 1], here.at_y(to))
    total = a3[y]
    for j in range(NY - 1):
        arrived(r3.at[j], r_3.at[j])
        total = total + r3[j]
    fin[...] = total[:2]
    d_out[...] = total[2]

    m_out[y] = total[:2]
    for j in FAR_FIRST:
        send(fin, m_out.at[y], s_f.at[j - 1], r_f.at[j - 1], here.at_y(mod(y + j, NY)))
    for j in range(1, NY):
        arrived(m_out.at[mod(y - j + NY, NY)], r_f.at[j - 1])

    @pl.loop(0, NZ)
    def _(i):
        for k, (src, dst) in enumerate(parts(target(i), 1 - c, high)):
            arrived(src, s_raw_s.at[i, k])
        for j in range(NX - 1):
            arrived(ta.at[0, 0], s_a.at[j, i])

    @pl.loop(0, NZ - 1)
    def _(i):
        for xx in range(NX):
            arrived(tg.at[0, 0], s_g.at[i, xx])
        arrived(ta.at[0, 0], s_z.at[i])
        arrived(a3.at[0], s_3.at[i])
        arrived(fin, s_f.at[i])

    for j in range(NX - 1):
        arrived(tg.at[0, 0], s_x.at[j])


def gram_sums(hid, grd):
    dma = pltpu.SemaphoreType.DMA
    tile = (8, BLK)
    vm = pltpu.VMEM
    shapes = ((NZ, 2), (NX - 1, NZ), (NZ - 1,), (NZ - 1, NX), (NX - 1,), (NY - 1,), (NY - 1,))
    return pl.pallas_call(
        gram_kernel,
        out_shape=(jax.ShapeDtypeStruct((NY, 2) + tile, F32), jax.ShapeDtypeStruct(tile, F32)),
        in_specs=[pl.BlockSpec(memory_space=pl.ANY)] * 2,
        out_specs=[pl.BlockSpec(memory_space=pltpu.VMEM)] * 2,
        scratch_shapes=[
            vm((256, 8192), BF16),
            vm((NZ, NX, NY + 1) + tile, F32),
            vm((NZ, NX, NY) + tile, F32),
            vm((NZ, NY + 1) + tile, F32),
            vm((NZ, NY + 1) + tile, F32),
            vm((NZ, NY + 1) + tile, F32),
            vm((NZ - 1, NY + 1) + tile, F32),
            vm((NZ - 1, NX, NY) + tile, F32),
            vm((NX - 1, NY) + tile, F32),
            vm((NY, 3) + tile, F32),
            vm((NY - 1, 3) + tile, F32),
            vm((2,) + tile, F32),
            dma((NZ, 2)),
        ] + [dma(shape) for shape in shapes for _ in range(2)],
        compiler_params=pltpu.CompilerParams(
            collective_id=0, has_side_effects=True, vmem_limit_bytes=62 * 2**20
        ),
        cost_estimate=pl.CostEstimate(flops=2 * 64 * 256 * BLK * BLK, bytes_accessed=4 * 2**20, transcendentals=0),
        name="gram_sums",
    )(hid, grd)


def split3(value):
    high = value.astype(BF16)
    rest = value - high.astype(F32)
    mid = rest.astype(BF16)
    return high, mid, (rest - mid.astype(F32)).astype(BF16)


def product(left, right, fine):
    lh, lm, ll = split3(left)
    rh, rm, rl = split3(right)

    def dot(a, b):
        return jnp.dot(a, b, preferred_element_type=F32)

    if not fine:
        return dot(jnp.concatenate((lh, lm), axis=1), jnp.concatenate((rh, rh), axis=0)) + dot(lh, rm)
    small = dot(jnp.concatenate((lm, ll), axis=1), jnp.concatenate((rm, rh), axis=0))
    middle = dot(jnp.concatenate((lh, lm), axis=1), jnp.concatenate((rm, rh), axis=0))
    large = dot(jnp.concatenate((lh, lh), axis=1), jnp.concatenate((rh, rl), axis=0))
    return large + (middle + small)


def newton_kernel(token_total, m_hbm, d_hbm, x_hbm, m_ref, d_ref, x_ref, sem):
    loads = [pltpu.make_async_copy(m_hbm, m_ref, sem.at[0]), pltpu.make_async_copy(d_hbm, d_ref, sem.at[1])]
    for load in loads:
        load.start()
    for load in loads:
        load.wait()
    second = mod(Place().y, 2) == 1
    packed = m_ref[...].reshape(BLK, BLK)
    extra = jnp.broadcast_to(d_ref[...][None], (16, 8, BLK)).reshape(BLK, BLK)
    row = lax.broadcasted_iota(jnp.int32, (BLK, BLK), 0)
    col = lax.broadcasted_iota(jnp.int32, (BLK, BLK), 1)
    turned = packed.T
    first_block = jnp.where(row // 8 <= col // 8, packed, turned)
    second_block = jnp.where(row // 8 == col // 8, extra, jnp.where(row // 8 > col // 8, packed, turned))
    sums = jnp.where(second, second_block, first_block)
    identity = jnp.where(row == col, 1.0, 0.0)
    factor = sums / token_total + DAMPING * identity
    bound = jnp.max(jnp.sum(jnp.abs(factor), axis=1, keepdims=True), axis=0, keepdims=True)
    both = jnp.concatenate((factor / bound, identity / bound), axis=1)

    def refine(fine):
        return lambda step, both: 2.0 * both - product(both[:, :BLK], both, fine)

    both = lax.fori_loop(0, FINE, refine(True), both)
    both = lax.fori_loop(FINE, ITERS, refine(False), both)
    x_ref[...] = both[:, BLK:].astype(BF16)
    store = pltpu.make_async_copy(x_ref, x_hbm, sem.at[0])
    store.start()
    store.wait()


def newton(token_total, packed, extra):
    out = jax.ShapeDtypeStruct((BLK, BLK), BF16)
    return pl.pallas_call(
        lambda *refs: newton_kernel(token_total, *refs),
        out_shape=out,
        in_specs=[pl.BlockSpec(memory_space=pl.ANY)] * 2,
        out_specs=pl.BlockSpec(memory_space=pl.ANY),
        scratch_shapes=[pltpu.VMEM(a.shape, a.dtype) for a in (packed, extra, out)] + [pltpu.SemaphoreType.DMA((2,))],
        compiler_params=pltpu.CompilerParams(vmem_limit_bytes=62 * 2**20),
        name="newton",
    )(packed, extra)


def spread_kernel(inv, owner_a, owner_g, r4, r5,
                  kept, es, er, s4, s_l, s_p, r_p, s_z, r_z, s_q, r_q, s_e, r_e, s_4, r_4, s_5, r_5):
    here = Place()
    x, y, z, c, yh, own = here.x, here.y, here.z, here.c, here.yh, here.own
    q = mod(y, 2)
    sib = here.other_core()
    beside = [here.at_y(mod(y + step, NY)) for step in (1, NY - 1)]

    barrier = pltpu.get_barrier_semaphore()
    onward, back = here.at_z(mod(z + 1, NZ)), here.at_z(mod(z + NZ - 1, NZ))
    for to in [sib, onward, back] + beside:
        pl.semaphore_signal(barrier, inc=1, device_id=to, device_id_type=MESH)
    for j in range(1, NX):
        pl.semaphore_signal(barrier, inc=1, device_id=here.at_x(mod(x + j, NX)), device_id_type=MESH)

    mine_here = pltpu.make_async_copy(inv.at[pl.ds(pl.multiple_of(32 * x, 32), 32)], kept.at[q, z, x], s_l)
    mine_here.start()
    pl.semaphore_wait(barrier, 1 + (NX - 1) + 2 + 2)
    for j in (2, 1, 3):
        to = mod(x + j, NX)
        send(inv.at[pl.ds(pl.multiple_of(32 * to, 32), 32)], kept.at[q, z, x],
             s_p.at[j - 1], r_p.at[j - 1], here.at_x(to))
    mine_here.wait()
    for j in range(1, NX):
        arrived(kept.at[q, z, mod(x - j + NX, NX)], r_p.at[j - 1])

    def along_z(zz, k, to):
        send(kept.at[q, zz], kept.at[q, zz], s_z.at[k], r_z.at[k], to)

    along_z(z, 0, onward)
    along_z(z, 4, back)

    def to_neighbours(zz, j):
        for k in range(2):
            half = kept.at[q, zz, pl.ds(2 * k, 2)]
            send(half, half, s_q.at[j, k], r_q.at[j, k], beside[k])

    to_neighbours(z, 0)

    def find_a(b, found):
        at = owner_a[b] - 3 * own
        return tuple(jnp.where(at == k, b, found[k]) for k in range(3))

    def find_g(b, found):
        return jnp.where(owner_g[b] == own, b, found)

    zero = jnp.int32(0)
    slot_a = lax.fori_loop(0, 96, find_a, (zero, zero, zero))
    slot_g = lax.fori_loop(0, 32, find_g, zero)

    def at_a(b):
        return mod(b, 2), lax.div(mod(b, 48), 6), lax.div(mod(b, 6), 2)

    def at_g(b):
        return mod(b, 2), lax.div(mod(b, 16), 2), 3

    def entry(core, k):
        if k == 3:
            return lax.div(slot_g, 16), at_g(slot_g)
        block = jnp.where(core == 0, slot_a[k], 3 * own + k)
        return lax.div(block, 48), at_a(block)

    mine = [entry(c, k) for k in range(4)]
    theirs = [entry(1 - c, k) for k in range(4)]
    for j in range(1, 5):
        zz = mod(z - j + NZ, NZ)
        arrived(kept.at[q, zz], r_z.at[j - 1])
        if j < 4:
            along_z(zz, j, onward)
        to_neighbours(zz, j)
        if j < 4:
            zz = mod(z + j, NZ)
            arrived(kept.at[q, zz], r_z.at[3 + j])
            if j < 3:
                along_z(zz, 4 + j, back)
            to_neighbours(zz, NZ - j)
    for j in range(NZ):
        zz = mod(z - j + NZ, NZ)
        for k in range(2):
            arrived(kept.at[1 - q, zz, pl.ds(2 * k, 2)], r_q.at[j, k])

    for k in range(4):
        es[k] = kept[theirs[k][1]]
    for m in range(2):
        for k in range(2):
            es[4 + 2 * m + k] = kept[at_g(8 * (2 * c + m) + 4 * yh + 2 * (1 - c) + k)]
    send(es, er, s_e.at[0], r_e.at[0], sib)
    values = [kept[mine[k][1]] for k in range(4)]
    arrived(er, r_e.at[0])
    values = [jnp.where(mine[k][0] == c, values[k], er[k]) for k in range(4)]
    for j in range(1, NX + 1):
        to = mod(x + j, NX)
        for k in range(4):
            s4[to, k] = values[k]
        for k in range(2):
            own_half = kept[at_g(8 * to + 4 * yh + 2 * c + k)]
            s4[to, 4 + k] = jnp.where(lax.div(to, 2) == c, own_half, er[4 + 2 * mod(to, 2) + k])
        if j < NX:
            send(s4.at[to], r4.at[x], s_4.at[j - 1], r_4.at[j - 1], here.at_x(to))
    r4[x] = s4[x]
    send(s4.at[x, pl.ds(0, 4)], r5.at[x], s_5.at[0], r_5.at[0], sib)
    for j in range(1, NX):
        frm = mod(x - j + NX, NX)
        arrived(r4.at[frm], r_4.at[j - 1])
        send(r4.at[frm, pl.ds(0, 4)], r5.at[frm], s_5.at[j], r_5.at[j], sib)
    for j in range(NX):
        arrived(r5.at[mod(x - j + NX, NX)], r_5.at[j])

    for j in range(NZ):
        for k in range(2):
            arrived(kept.at[q, j, pl.ds(2 * k, 2)], s_q.at[j, k])
    for j in range(NZ - 1):
        arrived(kept.at[q, z], s_z.at[j])
    for j in range(NX - 1):
        arrived(kept.at[q, z, x], s_p.at[j])
        arrived(s4.at[j], s_4.at[j])
    arrived(es, s_e.at[0])
    for j in range(NX):
        arrived(r5.at[j], s_5.at[j])


def spread(inv, owner_a, owner_g):
    dma = pltpu.SemaphoreType.DMA
    vm = pltpu.VMEM
    piece = (32, BLK)
    shapes = ((NX - 1,), (NZ - 1,), (NZ, 2), (1,), (NX - 1,), (NX,))
    return pl.pallas_call(
        spread_kernel,
        out_shape=(jax.ShapeDtypeStruct((NX, 6) + piece, BF16), jax.ShapeDtypeStruct((NX, 4) + piece, BF16)),
        in_specs=[pl.BlockSpec(memory_space=pl.ANY)] + [pl.BlockSpec(memory_space=pltpu.SMEM)] * 2,
        out_specs=[pl.BlockSpec(memory_space=pltpu.VMEM)] * 2,
        scratch_shapes=[
            vm((2, NZ, NX) + piece, BF16), vm((8,) + piece, BF16), vm((8,) + piece, BF16), vm((NX, 6) + piece, BF16), dma,
        ] + [dma(shape) for shape in shapes for _ in range(2)],
        compiler_params=pltpu.CompilerParams(
            collective_id=1, has_side_effects=True, vmem_limit_bytes=62 * 2**20
        ),
        name="spread_inverses",
    )(inv, owner_a, owner_g)


def apply_kernel(r4_hbm, r5_hbm, w_hbm, a_hbm, g_hbm, p_hbm, r4, r5, w, a_out, g_out, p_out, s_in, s_out):
    c = Place().c
    loads = [
        pltpu.make_async_copy(src, dst, s_in.at[k])
        for k, (src, dst) in enumerate(((r4_hbm, r4), (r5_hbm, r5), (w_hbm, w)))
    ]
    for load in loads:
        load.start()
    for load in loads:
        load.wait()

    def whole(ref, k):
        return ref[:, k].reshape(BLK, BLK)

    mine = [whole(r4, k) for k in range(6)]
    theirs = [whole(r5, k) for k in range(4)]
    core0 = c == 0
    stores = []

    def store(src, dst):
        stores.append(pltpu.make_async_copy(src, dst, s_out.at[len(stores)]))
        stores[-1].start()

    for k in range(3):
        placed = jnp.where(core0, theirs[k], mine[k])
        rows = pl.ds(BLK * k, BLK)
        left = jnp.dot(placed, w[rows, :], preferred_element_type=F32).astype(BF16)
        for m in range(2):
            cols = slice(BLK * m, BLK * (m + 1))
            p_out[rows, cols] = jnp.dot(left[:, cols], mine[4 + m], preferred_element_type=F32)
        store(p_out.at[rows], p_hbm.at[rows])
    for k in range(3):
        a_out[k] = jnp.where(core0, mine[k], theirs[k])
    store(a_out, a_hbm)
    g_out[0] = mine[3]
    store(g_out, g_hbm)
    for each in stores:
        each.wait()


def apply_inverses(r4, r5, w):
    outs = (
        jax.ShapeDtypeStruct((3, BLK, BLK), BF16),
        jax.ShapeDtypeStruct((1, BLK, BLK), BF16),
        jax.ShapeDtypeStruct(w.shape, F32),
    )
    return pl.pallas_call(
        apply_kernel,
        out_shape=outs,
        in_specs=[pl.BlockSpec(memory_space=pl.ANY)] * 3,
        out_specs=[pl.BlockSpec(memory_space=pl.ANY)] * 3,
        scratch_shapes=[pltpu.VMEM(a.shape, a.dtype) for a in (r4, r5, w) + outs]
        + [pltpu.SemaphoreType.DMA((3,)), pltpu.SemaphoreType.DMA((5,))],
        compiler_params=pltpu.CompilerParams(vmem_limit_bytes=62 * 2**20),
        name="apply_inverses",
    )(r4, r5, w)


def on_device(hidden_act, out_grad, weight_grad, owner_a, owner_g):
    token_total = hidden_act.shape[0] * lax.axis_size("own") * lax.axis_size("dp")
    packed, extra = gram_sums(hidden_act, out_grad)
    inverse = newton(token_total, packed, extra)
    return apply_inverses(*spread(inverse, owner_a, owner_g), weight_grad)


def solution(mesh):
    placed = (P(("dp", "own"), None), P(("dp", "own"), None), P("own", "dp"), P(), P())
    return jax.shard_map(
        on_device,
        mesh=mesh,
        in_specs=placed,
        out_specs=(P("own", None, None), P("own", None, None), P("own", "dp")),
        check_vma=False,
    )
```

```python
import jax
import jax.numpy as jnp
from jax import lax
from jax.experimental import pallas as pl
from jax.experimental.pallas import tpu as pltpu
from jax.sharding import PartitionSpec as P

BLK = 128
ITERS = 14
FINE = 4
DAMPING = 0.05
NX, NY, NZ, NYL = 4, 8, 8, 4
MESH = pl.DeviceIdType.MESH
F32 = jnp.float32
BF16 = jnp.bfloat16


FAR_FIRST = (4, 3, 5, 2, 6, 1, 7)


def mod(value, n):
    return value % n if isinstance(value, int) else lax.rem(value, n)


class Place:
    def __init__(self):
        self.dp, self.own = lax.axis_index("dp"), lax.axis_index("own")
        self.x, self.c = lax.div(self.dp, 4), mod(self.dp, 2)
        self.yh = mod(lax.div(self.dp, 2), 2)
        self.z, self.yl = lax.div(self.own, NYL), mod(self.own, NYL)
        self.y = self.yh * NYL + self.yl

    def at_x(self, to):
        return (self.dp + 4 * (to - self.x), self.own)

    def at_y(self, to):
        return (self.dp + 2 * (lax.div(to, NYL) - self.yh), self.own + mod(to, NYL) - self.yl)

    def at_z(self, to):
        return (self.dp, self.own + NYL * (to - self.z))

    def other_core(self):
        return (self.dp + 1 - 2 * self.c, self.own)


def send(src, dst, send_sem, recv_sem, to):
    copy = pltpu.make_async_remote_copy(
        src_ref=src, dst_ref=dst, send_sem=send_sem, recv_sem=recv_sem,
        device_id=to, device_id_type=MESH,
    )
    copy.start()


def arrived(ref, sem):
    pltpu.make_async_copy(ref, ref, sem).wait()


def gram_kernel(hid, grd, m_out, d_out,
                raw, ta, tb, tg, ra, rb, rg, a2, b2, g2, ra2, rb2, rg2, a3, x3, ra3, rx3, fin,
                s_loc, s_raw_s, s_raw_r, s_a, r_a, s_b, r_b, s_g, r_g,
                s_a2, r_a2, s_b2, r_b2, s_g2, r_g2, s_a3, r_a3, s_x3, r_x3, s_f, r_f):
    here = Place()
    x, y, z, c = here.x, here.y, here.z, here.c
    sib = here.other_core()

    barrier = pltpu.get_barrier_semaphore()
    pl.semaphore_signal(barrier, inc=1, device_id=sib, device_id_type=MESH)
    for j in range(1, NX):
        pl.semaphore_signal(barrier, inc=1, device_id=here.at_x(mod(x + j, NX)), device_id_type=MESH)
    for j in range(1, NY):
        pl.semaphore_signal(barrier, inc=1, device_id=here.at_y(mod(y + j, NY)), device_id_type=MESH)
    for j in range(1, NZ):
        pl.semaphore_signal(barrier, inc=1, device_id=here.at_z(mod(z + j, NZ)), device_id_type=MESH)

    def halves(core, rows):
        return (
            (hid.at[:, pl.ds(pl.multiple_of(6144 * core, 128), 6144)], raw.at[rows, pl.ds(0, 6144)]),
            (grd.at[:, pl.ds(pl.multiple_of(2048 * core, 128), 2048)], raw.at[rows, pl.ds(6144, 2048)]),
        )

    low, high = pl.ds(0, 128), pl.ds(128, 128)
    own_part = [pltpu.make_async_copy(src, dst, s_loc.at[k]) for k, (src, dst) in enumerate(halves(c, low))]
    for part in own_part:
        part.start()
    pl.semaphore_wait(barrier, 1 + (NX - 1) + (NY - 1) + (NZ - 1))
    for k, (src, dst) in enumerate(halves(1 - c, high)):
        send(src, dst, s_raw_s.at[k], s_raw_r.at[k], sib)

    row8 = lax.broadcasted_iota(jnp.int32, (BLK, BLK), 0) // 8
    col8 = lax.broadcasted_iota(jnp.int32, (BLK, BLK), 1) // 8
    upper = row8 <= col8
    middle = row8 == col8

    def gram(zz, k):
        at = 768 * zz + BLK * k if k < 6 else 6144 + 256 * zz + BLK * (k - 6)
        cols = pl.ds(pl.multiple_of(at, BLK), BLK)
        tok = raw[:, cols]
        return lax.dot_general(tok, tok, (((0,), (0,)), ((), ())), preferred_element_type=F32)

    for part in own_part:
        part.wait()
    for k, (src, dst) in enumerate(halves(c, high)):
        arrived(dst, s_raw_r.at[k])

    def gram_step(i):
        zz = mod(z + 1 + i, NZ)
        for xx in range(NX):
            first = gram(zz, 2 * xx)
            second = gram(zz, 2 * xx + 1)
            packed = jnp.where(upper, first, second).reshape(NY, 2, 8, BLK)
            extra = jnp.sum(jnp.where(middle, second, 0.0).reshape(16, 8, BLK), axis=0)
            ta[xx, i, pl.ds(0, NY)] = packed[:, 0]
            ta[xx, i, NY] = extra
            if xx < 2:
                tb[:, i, xx] = packed[:, 1]
            else:
                tg[zz, xx - 2] = packed[:, 1]
        return zz

    @pl.loop(0, 4)
    def _(k):
        zz = gram_step(2 * k)
        send(tg.at[zz], rg.at[2 * k], s_g.at[2 * k], r_g.at[2 * k], here.at_z(zz))
        zz = gram_step(2 * k + 1)
        for j in (2, 1, 3):
            to = mod(x + j, NX)
            send(ta.at[to, pl.ds(2 * k, 2)], ra.at[j - 1, pl.ds(2 * k, 2)], s_a.at[j - 1, k], r_a.at[j - 1, k], here.at_x(to))

        @pl.when(k < 3)
        def _():
            send(tg.at[zz], rg.at[2 * k + 1], s_g.at[2 * k + 1], r_g.at[2 * k + 1], here.at_z(zz))

        @pl.when(k % 2 == 1)
        def _():
            half = k // 2
            for j in FAR_FIRST:
                to = mod(y + j, NY)
                send(tb.at[to, pl.ds(4 * half, 4)], rb.at[j - 1, pl.ds(4 * half, 4)],
                     s_b.at[j - 1, half], r_b.at[j - 1, half], here.at_y(to))

    @pl.loop(0, 4)
    def _(k):
        for j in range(NX - 1):
            arrived(ra.at[j, pl.ds(2 * k, 2)], r_a.at[j, k])
        for i in (2 * k, 2 * k + 1):
            zz = mod(z + 1 + i, NZ)
            total = ta[x, i]
            for j in range(NX - 1):
                total = total + ra[j, i]
            a2[zz] = total

            @pl.when(i < NZ - 1)
            def _():
                send(a2.at[zz], ra2.at[i], s_a2.at[i], r_a2.at[i], here.at_z(zz))

    for j in range(NZ - 1):
        arrived(rg.at[j], r_g.at[j])
    for k in range(2):
        total = tg[z, k]
        for j in range(NZ - 1):
            total = total + rg[j, k]
        for yy in range(NY):
            g2[yy, k] = total[yy]
    for j in FAR_FIRST:
        to = mod(y + j, NY)
        send(g2.at[to], rg2.at[j - 1], s_g2.at[j - 1], r_g2.at[j - 1], here.at_y(to))

    for j in range(NY - 1):
        for half in range(2):
            arrived(rb.at[j, pl.ds(4 * half, 4)], r_b.at[j, half])

    @pl.loop(0, NZ)
    def _(i):
        total = tb[y, i]
        for j in range(NY - 1):
            total = total + rb[j, i]
        b2[i] = total
        zz = mod(z + 1 + i, NZ)

        @pl.when(i < NZ - 1)
        def _():
            send(b2.at[i], rb2.at[i], s_b2.at[i], r_b2.at[i], here.at_z(zz))

    total = a2[z]
    for j in range(NZ - 1):
        arrived(ra2.at[j], r_a2.at[j])
        total = total + ra2[j]
    for yy in range(NY):
        a3[yy, 0] = total[yy]
        a3[yy, 1] = total[NY]
    for j in FAR_FIRST:
        to = mod(y + j, NY)
        send(a3.at[to], ra3.at[j - 1], s_a3.at[j - 1], r_a3.at[j - 1], here.at_y(to))

    total = g2[y]
    for j in range(NY - 1):
        arrived(rg2.at[j], r_g2.at[j])
        total = total + rg2[j]
    x3[2] = total[0]
    x3[3] = total[1]
    total = b2[NZ - 1]
    for j in range(NZ - 1):
        arrived(rb2.at[j], r_b2.at[j])
        total = total + rb2[j]
    x3[0] = total[0]
    x3[1] = total[1]
    for j in (2, 1, 3):
        to = mod(x + j, NX)
        send(x3.at[to], rx3.at[j - 1], s_x3.at[j - 1], r_x3.at[j - 1], here.at_x(to))

    total = a3[y]
    for j in range(NY - 1):
        arrived(ra3.at[j], r_a3.at[j])
        total = total + ra3[j]
    fin[0] = total[0]
    d_out[...] = total[1]
    total = x3[x]
    for j in range(NX - 1):
        arrived(rx3.at[j], r_x3.at[j])
        total = total + rx3[j]
    fin[1] = total

    m_out[y] = fin[...]
    for j in FAR_FIRST:
        to = mod(y + j, NY)
        send(fin, m_out.at[y], s_f.at[j - 1], r_f.at[j - 1], here.at_y(to))
    for j in range(1, NY):
        arrived(m_out.at[mod(y - j + NY, NY)], r_f.at[j - 1])

    for k, (src, dst) in enumerate(halves(1 - c, high)):
        arrived(src, s_raw_s.at[k])
    for j in range(NX - 1):
        for k in range(4):
            arrived(ta.at[0, pl.ds(2 * k, 2)], s_a.at[j, k])
    for j in range(NZ - 1):
        arrived(tg.at[j], s_g.at[j])
        arrived(a2.at[j], s_a2.at[j])
        arrived(b2.at[j], s_b2.at[j])
    for j in range(NY - 1):
        for half in range(2):
            arrived(tb.at[j, pl.ds(4 * half, 4)], s_b.at[j, half])
        arrived(g2.at[j], s_g2.at[j])
        arrived(a3.at[j], s_a3.at[j])
        arrived(fin, s_f.at[j])
    for j in range(NX - 1):
        arrived(x3.at[j], s_x3.at[j])


def gram_sums(hid, grd):
    dma = pltpu.SemaphoreType.DMA
    tile = (8, BLK)
    vm = pltpu.VMEM
    return pl.pallas_call(
        gram_kernel,
        out_shape=(jax.ShapeDtypeStruct((NY, 2) + tile, F32), jax.ShapeDtypeStruct(tile, F32)),
        in_specs=[pl.BlockSpec(memory_space=pl.ANY)] * 2,
        out_specs=[pl.BlockSpec(memory_space=pltpu.VMEM)] * 2,
        scratch_shapes=[
            vm((256, 8192), BF16),
            vm((NX, NZ, NY + 1) + tile, F32),
            vm((NY, NZ, 2) + tile, F32),
            vm((NZ, 2, NY) + tile, F32),
            vm((NX - 1, NZ, NY + 1) + tile, F32),
            vm((NY - 1, NZ, 2) + tile, F32),
            vm((NZ - 1, 2, NY) + tile, F32),
            vm((NZ, NY + 1) + tile, F32),
            vm((NZ, 2) + tile, F32),
            vm((NY, 2) + tile, F32),
            vm((NZ - 1, NY + 1) + tile, F32),
            vm((NZ - 1, 2) + tile, F32),
            vm((NY - 1, 2) + tile, F32),
            vm((NY, 2) + tile, F32),
            vm((NX,) + tile, F32),
            vm((NY - 1, 2) + tile, F32),
            vm((NX - 1,) + tile, F32),
            vm((2,) + tile, F32),
            dma((2,)), dma((2,)), dma((2,)),
            dma((NX - 1, 4)), dma((NX - 1, 4)),
            dma((NY - 1, 2)), dma((NY - 1, 2)),
            dma((NZ - 1,)), dma((NZ - 1,)),
            dma((NZ - 1,)), dma((NZ - 1,)),
            dma((NZ - 1,)), dma((NZ - 1,)),
            dma((NY - 1,)), dma((NY - 1,)),
            dma((NY - 1,)), dma((NY - 1,)),
            dma((NX - 1,)), dma((NX - 1,)),
            dma((NY - 1,)), dma((NY - 1,)),
        ],
        compiler_params=pltpu.CompilerParams(
            collective_id=0, has_side_effects=True, vmem_limit_bytes=62 * 2**20
        ),
        cost_estimate=pl.CostEstimate(flops=2 * 64 * 256 * BLK * BLK, bytes_accessed=4 * 2**20, transcendentals=0),
        name="gram_sums",
    )(hid, grd)


def split3(value):
    high = value.astype(BF16)
    rest = value - high.astype(F32)
    mid = rest.astype(BF16)
    return high, mid, (rest - mid.astype(F32)).astype(BF16)


def product(left, right, fine):
    lh, lm, ll = split3(left)
    rh, rm, rl = split3(right)

    def dot(a, b):
        return jnp.dot(a, b, preferred_element_type=F32)

    if not fine:
        return dot(jnp.concatenate((lh, lm), axis=1), jnp.concatenate((rh, rh), axis=0)) + dot(lh, rm)
    small = dot(jnp.concatenate((lm, ll), axis=1), jnp.concatenate((rm, rh), axis=0))
    middle = dot(jnp.concatenate((lh, lm), axis=1), jnp.concatenate((rm, rh), axis=0))
    large = dot(jnp.concatenate((lh, lh), axis=1), jnp.concatenate((rh, rl), axis=0))
    return large + (middle + small)


def newton_kernel(token_total, m_hbm, d_hbm, x_hbm, m_ref, d_ref, x_ref, sem):
    loads = [pltpu.make_async_copy(m_hbm, m_ref, sem.at[0]), pltpu.make_async_copy(d_hbm, d_ref, sem.at[1])]
    for load in loads:
        load.start()
    for load in loads:
        load.wait()
    second = mod(Place().y, 2) == 1
    packed = m_ref[...].reshape(BLK, BLK)
    extra = jnp.broadcast_to(d_ref[...][None], (16, 8, BLK)).reshape(BLK, BLK)
    row = lax.broadcasted_iota(jnp.int32, (BLK, BLK), 0)
    col = lax.broadcasted_iota(jnp.int32, (BLK, BLK), 1)
    turned = packed.T
    first_block = jnp.where(row // 8 <= col // 8, packed, turned)
    second_block = jnp.where(row // 8 == col // 8, extra, jnp.where(row // 8 > col // 8, packed, turned))
    sums = jnp.where(second, second_block, first_block)
    identity = jnp.where(row == col, 1.0, 0.0)
    factor = sums / token_total + DAMPING * identity
    bound = jnp.max(jnp.sum(jnp.abs(factor), axis=1, keepdims=True), axis=0, keepdims=True)
    both = jnp.concatenate((factor / bound, identity / bound), axis=1)

    def refine(fine):
        return lambda step, both: 2.0 * both - product(both[:, :BLK], both, fine)

    both = lax.fori_loop(0, FINE, refine(True), both)
    both = lax.fori_loop(FINE, ITERS, refine(False), both)
    x_ref[...] = both[:, BLK:].astype(BF16)
    store = pltpu.make_async_copy(x_ref, x_hbm, sem.at[0])
    store.start()
    store.wait()


def newton(token_total, packed, extra):
    out = jax.ShapeDtypeStruct((BLK, BLK), BF16)
    return pl.pallas_call(
        lambda *refs: newton_kernel(token_total, *refs),
        out_shape=out,
        in_specs=[pl.BlockSpec(memory_space=pl.ANY)] * 2,
        out_specs=pl.BlockSpec(memory_space=pl.ANY),
        scratch_shapes=[pltpu.VMEM(a.shape, a.dtype) for a in (packed, extra, out)] + [pltpu.SemaphoreType.DMA((2,))],
        compiler_params=pltpu.CompilerParams(vmem_limit_bytes=62 * 2**20),
        name="newton",
    )(packed, extra)


def spread_kernel(inv, owner_a, owner_g, r4, r5,
                  kept, es, er, s4, s_l, s_p, r_p, s_z, r_z, s_q, r_q, s_e, r_e, s_4, r_4, s_5, r_5):
    here = Place()
    x, y, z, c, yh, own = here.x, here.y, here.z, here.c, here.yh, here.own
    q = mod(y, 2)
    sib = here.other_core()
    beside = [here.at_y(mod(y + step, NY)) for step in (1, NY - 1)]

    barrier = pltpu.get_barrier_semaphore()
    for to in [sib] + beside:
        pl.semaphore_signal(barrier, inc=1, device_id=to, device_id_type=MESH)
    for j in range(1, NX):
        pl.semaphore_signal(barrier, inc=1, device_id=here.at_x(mod(x + j, NX)), device_id_type=MESH)
    for j in range(1, NZ):
        pl.semaphore_signal(barrier, inc=1, device_id=here.at_z(mod(z + j, NZ)), device_id_type=MESH)

    mine_here = pltpu.make_async_copy(inv.at[pl.ds(pl.multiple_of(32 * x, 32), 32)], kept.at[q, z, x], s_l)
    mine_here.start()
    pl.semaphore_wait(barrier, 1 + (NX - 1) + 2 + (NZ - 1))
    for j in (2, 1, 3):
        to = mod(x + j, NX)
        send(inv.at[pl.ds(pl.multiple_of(32 * to, 32), 32)], kept.at[q, z, x],
             s_p.at[j - 1], r_p.at[j - 1], here.at_x(to))
    mine_here.wait()
    for j in range(1, NX):
        arrived(kept.at[q, z, mod(x - j + NX, NX)], r_p.at[j - 1])
    for j in FAR_FIRST:
        send(kept.at[q, z], kept.at[q, z], s_z.at[j - 1], r_z.at[j - 1], here.at_z(mod(z + j, NZ)))

    def to_neighbours(zz, j):
        for k in range(2):
            half = kept.at[q, zz, pl.ds(2 * k, 2)]
            send(half, half, s_q.at[j, k], r_q.at[j, k], beside[k])

    to_neighbours(z, 0)

    def find_a(b, found):
        at = owner_a[b] - 3 * own
        return tuple(jnp.where(at == k, b, found[k]) for k in range(3))

    def find_g(b, found):
        return jnp.where(owner_g[b] == own, b, found)

    zero = jnp.int32(0)
    slot_a = lax.fori_loop(0, 96, find_a, (zero, zero, zero))
    slot_g = lax.fori_loop(0, 32, find_g, zero)

    def at_a(b):
        return mod(b, 2), lax.div(mod(b, 48), 6), lax.div(mod(b, 6), 2)

    def at_g(b):
        return mod(b, 2), lax.div(mod(b, 16), 2), 3

    def entry(core, k):
        if k == 3:
            return lax.div(slot_g, 16), at_g(slot_g)
        block = jnp.where(core == 0, slot_a[k], 3 * own + k)
        return lax.div(block, 48), at_a(block)

    mine = [entry(c, k) for k in range(4)]
    theirs = [entry(1 - c, k) for k in range(4)]
    for j in FAR_FIRST:
        zz = mod(z - j + NZ, NZ)
        arrived(kept.at[q, zz], r_z.at[j - 1])
        to_neighbours(zz, j)
    for j in range(NZ):
        zz = mod(z - j + NZ, NZ)
        for k in range(2):
            arrived(kept.at[1 - q, zz, pl.ds(2 * k, 2)], r_q.at[j, k])

    for k in range(4):
        es[k] = kept[theirs[k][1]]
    for m in range(2):
        for k in range(2):
            es[4 + 2 * m + k] = kept[at_g(8 * (2 * c + m) + 4 * yh + 2 * (1 - c) + k)]
    send(es, er, s_e.at[0], r_e.at[0], sib)
    values = [kept[mine[k][1]] for k in range(4)]
    arrived(er, r_e.at[0])
    values = [jnp.where(mine[k][0] == c, values[k], er[k]) for k in range(4)]
    for j in range(1, NX + 1):
        to = mod(x + j, NX)
        for k in range(4):
            s4[to, k] = values[k]
        for k in range(2):
            own_half = kept[at_g(8 * to + 4 * yh + 2 * c + k)]
            s4[to, 4 + k] = jnp.where(lax.div(to, 2) == c, own_half, er[4 + 2 * mod(to, 2) + k])
        if j < NX:
            send(s4.at[to], r4.at[x], s_4.at[j - 1], r_4.at[j - 1], here.at_x(to))
    r4[x] = s4[x]
    send(s4.at[x, pl.ds(0, 4)], r5.at[x], s_5.at[0], r_5.at[0], sib)
    for j in range(1, NX):
        frm = mod(x - j + NX, NX)
        arrived(r4.at[frm], r_4.at[j - 1])
        send(r4.at[frm, pl.ds(0, 4)], r5.at[frm], s_5.at[j], r_5.at[j], sib)
    for j in range(NX):
        arrived(r5.at[mod(x - j + NX, NX)], r_5.at[j])

    for j in range(NZ):
        for k in range(2):
            arrived(kept.at[q, j, pl.ds(2 * k, 2)], s_q.at[j, k])
    for j in range(NZ - 1):
        arrived(kept.at[q, z], s_z.at[j])
    for j in range(NX - 1):
        arrived(kept.at[q, z, x], s_p.at[j])
        arrived(s4.at[j], s_4.at[j])
    arrived(es, s_e.at[0])
    for j in range(NX):
        arrived(r5.at[j], s_5.at[j])


def spread(inv, owner_a, owner_g):
    dma = pltpu.SemaphoreType.DMA
    vm = pltpu.VMEM
    piece = (32, BLK)
    shapes = ((NX - 1,), (NZ - 1,), (NZ, 2), (1,), (NX - 1,), (NX,))
    return pl.pallas_call(
        spread_kernel,
        out_shape=(jax.ShapeDtypeStruct((NX, 6) + piece, BF16), jax.ShapeDtypeStruct((NX, 4) + piece, BF16)),
        in_specs=[pl.BlockSpec(memory_space=pl.ANY)] + [pl.BlockSpec(memory_space=pltpu.SMEM)] * 2,
        out_specs=[pl.BlockSpec(memory_space=pltpu.VMEM)] * 2,
        scratch_shapes=[
            vm((2, NZ, NX) + piece, BF16), vm((8,) + piece, BF16), vm((8,) + piece, BF16), vm((NX, 6) + piece, BF16), dma,
        ] + [dma(shape) for shape in shapes for _ in range(2)],
        compiler_params=pltpu.CompilerParams(
            collective_id=1, has_side_effects=True, vmem_limit_bytes=62 * 2**20
        ),
        name="spread_inverses",
    )(inv, owner_a, owner_g)


def apply_kernel(r4_hbm, r5_hbm, w_hbm, a_hbm, g_hbm, p_hbm, r4, r5, w, a_out, g_out, p_out, s_in, s_out):
    c = Place().c
    loads = [
        pltpu.make_async_copy(src, dst, s_in.at[k])
        for k, (src, dst) in enumerate(((r4_hbm, r4), (r5_hbm, r5), (w_hbm, w)))
    ]
    for load in loads:
        load.start()
    for load in loads:
        load.wait()

    def whole(ref, k):
        return ref[:, k].reshape(BLK, BLK)

    mine = [whole(r4, k) for k in range(6)]
    theirs = [whole(r5, k) for k in range(4)]
    core0 = c == 0
    stores = []

    def store(src, dst):
        stores.append(pltpu.make_async_copy(src, dst, s_out.at[len(stores)]))
        stores[-1].start()

    for k in range(3):
        placed = jnp.where(core0, theirs[k], mine[k])
        rows = pl.ds(BLK * k, BLK)
        left = jnp.dot(placed, w[rows, :], preferred_element_type=F32).astype(BF16)
        for m in range(2):
            cols = slice(BLK * m, BLK * (m + 1))
            p_out[rows, cols] = jnp.dot(left[:, cols], mine[4 + m], preferred_element_type=F32)
        store(p_out.at[rows], p_hbm.at[rows])
    for k in range(3):
        a_out[k] = jnp.where(core0, mine[k], theirs[k])
    store(a_out, a_hbm)
    g_out[0] = mine[3]
    store(g_out, g_hbm)
    for each in stores:
        each.wait()


def apply_inverses(r4, r5, w):
    outs = (
        jax.ShapeDtypeStruct((3, BLK, BLK), BF16),
        jax.ShapeDtypeStruct((1, BLK, BLK), BF16),
        jax.ShapeDtypeStruct(w.shape, F32),
    )
    return pl.pallas_call(
        apply_kernel,
        out_shape=outs,
        in_specs=[pl.BlockSpec(memory_space=pl.ANY)] * 3,
        out_specs=[pl.BlockSpec(memory_space=pl.ANY)] * 3,
        scratch_shapes=[pltpu.VMEM(a.shape, a.dtype) for a in (r4, r5, w) + outs]
        + [pltpu.SemaphoreType.DMA((3,)), pltpu.SemaphoreType.DMA((5,))],
        compiler_params=pltpu.CompilerParams(vmem_limit_bytes=62 * 2**20),
        name="apply_inverses",
    )(r4, r5, w)


def on_device(hidden_act, out_grad, weight_grad, owner_a, owner_g):
    token_total = hidden_act.shape[0] * lax.axis_size("own") * lax.axis_size("dp")
    packed, extra = gram_sums(hidden_act, out_grad)
    inverse = newton(token_total, packed, extra)
    return apply_inverses(*spread(inverse, owner_a, owner_g), weight_grad)


def solution(mesh):
    placed = (P(("dp", "own"), None), P(("dp", "own"), None), P("own", "dp"), P(), P())
    return jax.shard_map(
        on_device,
        mesh=mesh,
        in_specs=placed,
        out_specs=(P("own", None, None), P("own", None, None), P("own", "dp")),
        check_vma=False,
    )
```
